32 devices in a mesh: tm: 1, series: 32 (over z, y, x, core).
Axes of the slice: x: 2, y: 2, z: 4, core: 2. Of those that a mesh axis runs over, the one named last changes fastest.
Arguments:
- inputs: bfloat16 [64, 512, 512], P('series', 'tm'), may hold values from -6 to 6
- cotangent: bfloat16 [64, 512, 512], P('series', 'tm'), may hold values from -6 to 6
- taps: int32 [3], replicated, may hold values from 0 to 128, as said below
- weight: float32 [1536, 512], P('series'), may hold values from -0.15625 to 0.15625
- moment_one: float32 [1536, 512], P('series'), may hold values from -10 to 10
- second_moment_state: float32 [1536, 512], P('series'), may hold values from 1 to 100
Outputs:
- grad_input: bfloat16 [64, 512, 512], P('series', 'tm')
- new_weight: float32 [1536, 512], P('series')
- new_moment_one: float32 [1536, 512], P('series')
- new_moment_two: float32 [1536, 512], P('series')
The draws below stay inside these ranges and needn't reach their ends.
Inputs may be any that keep to these rules, and one draw needn't show every extreme that they name: taps[0] is 0, taps[2] is 128, and taps[1] lies strictly between them.
All inputs are finite; a program needn't handle non-finite values.
Results may differ from the reference program's by a relative error of at most 0.0045.
Values may be sent and summed in bfloat16 or wider, within the bound.
A program may use at most 64 MiB of HBM per device.

```python
import math
import jax
import jax.numpy as jnp
from jax import lax

C = 512
KERNEL_TAPS = 3
DILATION_GAP = 64
SERIES = 64
WINDOW = 512


def draw_taps(key, part):
    center_part = jax.random.randint(key, (1,), 1, 2 * DILATION_GAP).astype(jnp.int32)
    return jnp.concatenate([jnp.zeros((1,), jnp.int32), center_part, jnp.full((1,), 2 * DILATION_GAP, jnp.int32)])


def level_of(rng, extent, split, smallest, top_value):
    factor_of = 1.0
    for dim, shards_of in split:
        draws = jax.random.uniform(jax.random.fold_in(jax.random.fold_in(rng, 6), dim), (shards_of,), jnp.float32, smallest / len(split), top_value / len(split))
        factor_of = factor_of * jnp.repeat(jnp.exp(draws), extent[dim] // shards_of).reshape((-1,) + (1,) * (len(extent) - 1 - dim))
    return factor_of


def scatter_about(rng, shape, deviation, bound, split=(), held_as=jnp.bfloat16):
    array = deviation * jax.random.normal(rng, shape, jnp.float32)
    if split:
        array = array * level_of(rng, shape, split, -0.22, 0.18)
    return jnp.clip(array, -bound, bound).astype(held_as)


def setup_inputs(seed: int = 0) -> dict:
    seeds = jax.random.split(jax.random.key(seed), 7)
    return {
        "inputs": scatter_about(seeds[0], (SERIES, WINDOW, C), 1.0, 6.0, ((0, 32),)),
        "cotangent": scatter_about(seeds[1], (SERIES, WINDOW, C), 1.0, 6.0, ((0, 32),)),
        "taps": draw_taps(jax.random.fold_in(seeds[6], 71), 0),
        "weight": scatter_about(seeds[3], (KERNEL_TAPS * C, C), (KERNEL_TAPS * C) ** -0.5, 0.15625, ((0, 32),), jnp.float32),
        "moment_one": scatter_about(seeds[4], (KERNEL_TAPS * C, C), 2.0, 10.0, ((0, 32),), jnp.float32),
        "second_moment_state": jnp.clip(jnp.exp(math.log(100.0) - 4.6051702 * jax.random.uniform(seeds[5], (KERNEL_TAPS * C, C), jnp.float32) ** level_of(seeds[5], (KERNEL_TAPS * C, C), ((0, 32),), -0.2, 0.2)), 1.0, 100.0),
    }


def adamw(weight, grad, moment_one, second_moment_state):
    first = 0.9 * moment_one + 0.1 * grad
    second = 0.999 * second_moment_state + 0.001 * grad * grad
    unbiased_one = first / (1.0 - 0.9 ** 10)
    unbiased_two = second / (1.0 - 0.999 ** 10)
    updated = weight - 0.01 * (unbiased_one / (jnp.sqrt(unbiased_two) + 1e-08) + 0.1 * weight)
    return (updated, first, second)

def reference(inputs, cotangent, taps, weight, moment_one, second_moment_state):
    receptive_span = (KERNEL_TAPS - 1) * DILATION_GAP
    wcast = weight.astype(jnp.bfloat16)

    def one_series(grad, pair):
        seq_in, seq_up = pair
        extended = jnp.concatenate([jnp.zeros((receptive_span, C), jnp.bfloat16), seq_in], 0)
        stacked = jnp.concatenate([lax.dynamic_slice_in_dim(extended, (receptive_span - taps[k]).astype(jnp.int32), WINDOW, 0) for k in range(KERNEL_TAPS)], 1)
        pre = jnp.dot(stacked, wcast, preferred_element_type=jnp.float32)
        sig = jax.nn.sigmoid(pre)
        dpre = (seq_up.astype(jnp.float32) * (sig * (1.0 + pre * (1.0 - sig)))).astype(jnp.bfloat16)
        later = jnp.concatenate([dpre, jnp.zeros((receptive_span, C), jnp.bfloat16)], 0)
        result = seq_up.astype(jnp.float32)
        for k in range(KERNEL_TAPS):
            moved = lax.dynamic_slice_in_dim(later, taps[k].astype(jnp.int32), WINDOW, 0)
            result = result + jnp.dot(moved, wcast[k * C:(k + 1) * C].T, preferred_element_type=jnp.float32)
        grad = grad + lax.dot_general(stacked, dpre, (((0,), (0,)), ((), ())), preferred_element_type=jnp.float32)
        return (grad, result.astype(jnp.bfloat16))
    grad, grad_input = lax.scan(one_series, jnp.zeros((KERNEL_TAPS * C, C), jnp.float32), (inputs, cotangent))
    new_weight, new_moment_one, new_moment_two = adamw(weight, grad, moment_one, second_moment_state)
    return (grad_input, new_weight, new_moment_one, new_moment_two)
```

```python
import functools

import jax
import jax.numpy as jnp
from jax import lax
from jax.experimental import pallas as pl
from jax.experimental.pallas import tpu as pltpu
from jax.sharding import PartitionSpec as P

DILATION_GAP = 64


def passed_along(array, axis, by):
    size = lax.axis_size(axis)
    pairs = [(i, i + by) for i in range(size) if 0 <= i + by < size]
    return lax.ppermute(array, axis, pairs)


def adamw(weight, grad, moment_one, second_moment_state):
    first = 0.9 * moment_one + 0.1 * grad
    second = 0.999 * second_moment_state + 0.001 * grad * grad
    unbiased_one = first / (1.0 - 0.9**10)
    unbiased_two = second / (1.0 - 0.999**10)
    updated = weight - 0.01 * (unbiased_one / (jnp.sqrt(unbiased_two) + 1e-08) + 0.1 * weight)
    return (updated, first, second)


def body(inputs, cotangent, taps, weight, moment_one, second_moment_state):
    series_n, time_n, width = inputs.shape
    tap_count = taps.shape[0]
    receptive_span = (tap_count - 1) * DILATION_GAP
    rows = series_n * time_n
    wide = lax.all_gather(weight.astype(jnp.bfloat16), "series", axis=0, tiled=True)
    earlier = passed_along(inputs[:, time_n - receptive_span :, :], "tm", 1)
    extended = jnp.concatenate([earlier, inputs], 1)
    shifted = [
        lax.dynamic_slice_in_dim(extended, receptive_span - taps[k], time_n, 1)
        for k in range(tap_count)
    ]
    stacked = jnp.concatenate(shifted, 2).reshape(rows, tap_count * width)
    pre = jnp.dot(stacked, wide, preferred_element_type=jnp.float32)
    sig = jax.nn.sigmoid(pre)
    upstream = cotangent.reshape(rows, width)
    dpre_flat = (upstream.astype(jnp.float32) * (sig * (1.0 + pre * (1.0 - sig)))).astype(
        jnp.bfloat16
    )
    dpre = dpre_flat.reshape(series_n, time_n, width)
    ahead = passed_along(dpre[:, :receptive_span, :], "tm", -1)
    later = jnp.concatenate([dpre, ahead], 1)
    result = upstream.astype(jnp.float32)
    for k in range(tap_count):
        moved = lax.dynamic_slice_in_dim(later, taps[k], time_n, 1).reshape(rows, width)
        result = result + lax.dot_general(
            moved,
            wide[k * width : (k + 1) * width],
            (((1,), (1,)), ((), ())),
            preferred_element_type=jnp.float32,
        )
    grad_input = result.astype(jnp.bfloat16).reshape(series_n, time_n, width)
    grad_shard = lax.psum_scatter(
        lax.dot_general(
            stacked, dpre_flat, (((0,), (0,)), ((), ())), preferred_element_type=jnp.float32
        ),
        "series",
        scatter_dimension=0,
        tiled=True,
    )
    grad_shard = lax.psum(grad_shard, "tm")
    new_weight, new_moment_one, new_moment_two = adamw(
        weight, grad_shard, moment_one, second_moment_state
    )
    return (grad_input, new_weight, new_moment_one, new_moment_two)


MESH = pl.DeviceIdType.MESH
F32, BF16 = jnp.float32, jnp.bfloat16
PLANES, IN_PLANE = 4, 8


def fits(mesh):
    return mesh.shape["tm"] == 1 and mesh.shape["series"] == PLANES * IN_PLANE


def matmul(a, b):
    return jnp.dot(a, b, preferred_element_type=F32)


def matmul_t(a, b):
    return lax.dot_general(a, b, (((1,), (1,)), ((), ())), preferred_element_type=F32)


def kernel(
    taps_ref, x_hbm, cot_hbm, w_hbm, m1_hbm, m2_hbm,
    gi_hbm, nw_hbm, n1_hbm, n2_hbm,
    x, cot, w, m1, m2, gi, nw, n1, n2,
    wide, xs, xt, dk, g, s1, r1, s2a, s2b, r2a, r2b, s3a, s3b, r3a, r3b, s4, r4,
    load_sem, store_sem, ag_send, ag_recv, rs_send, rs_recv,
):
    series_n, time_n, width = x.shape
    span = 2 * DILATION_GAP
    rows = w.shape[0]
    half = width // 2
    tm = lax.axis_index("tm")
    me = lax.axis_index("series")
    core = lax.rem(me, 2)
    px_i = lax.rem(me // 2, 2)
    py_i = lax.rem(me // 4, 2)
    z = me // IN_PLANE

    def index(zz, yy, xx, cc):
        return ((zz * 2 + yy) * 2 + xx) * 2 + cc

    def block(zz, yy, xx, cc):
        return pl.ds(pl.multiple_of(index(zz, yy, xx, cc) * rows, 16), rows)

    to_x = (tm, index(z, py_i, 1 - px_i, core))
    to_y = (tm, index(z, 1 - py_i, px_i, core))
    to_c = (tm, index(z, py_i, px_i, 1 - core))
    to_z = [None] + [(tm, index(lax.rem(z + d, PLANES), py_i, px_i, core)) for d in (1, 2, 3)]

    loads = [
        pltpu.make_async_copy(src, dst, load_sem.at[i])
        for i, (src, dst) in enumerate(
            [(w_hbm, w), (x_hbm, x), (cot_hbm, cot), (m1_hbm, m1), (m2_hbm, m2)]
        )
    ]
    for c in loads:
        c.start()

    barrier = pltpu.get_barrier_semaphore()
    for dev in (to_x, to_y, to_c, *to_z[1:]):
        pl.semaphore_signal(barrier, inc=1, device_id=dev, device_id_type=MESH)

    loads[0].wait()
    own = block(z, py_i, px_i, core)
    wide[own, :] = w[...].astype(BF16)
    pl.semaphore_wait(barrier, 6)

    def start(src, dst, sems, k, dev):
        c = pltpu.make_async_remote_copy(
            src_ref=src, dst_ref=dst, send_sem=sems[0].at[k], recv_sem=sems[1].at[k],
            device_id=dev, device_id_type=MESH,
        )
        c.start()
        return c

    ag = (ag_send, ag_recv)
    rs = (rs_send, rs_recv)
    A, B, ALL = pl.ds(0, half), pl.ds(half, half), pl.ds(0, width)

    def pass_on(blk, cols, k, dev):
        return start(wide.at[blk, cols], wide.at[blk, cols], ag, k, dev)

    sent = []
    z_copies = [None] + [pass_on(own, ALL, d, to_z[d]) for d in (1, 2, 3)]
    sent += z_copies[1:]
    x1, y1 = [], []
    for j in range(PLANES):
        zj = lax.rem(z + PLANES - j, PLANES)
        if j:
            z_copies[j].wait_recv()
        blk = block(zj, py_i, px_i, core)
        x1.append(pass_on(blk, ALL, 4 + j, to_x))
        y1.append(pass_on(blk, ALL, 8 + j, to_y))
        sent.append(pass_on(blk, ALL, 12 + j, to_c))
        if j == 0:
            loads[1].wait()
            tap = taps_ref[1]
            row = lax.broadcasted_iota(jnp.int32, (time_n, time_n), 0)
            column = lax.broadcasted_iota(jnp.int32, (time_n, time_n), 1)
            back = jnp.where(column == row - tap, 1.0, 0.0).astype(BF16)
            for s in range(series_n):
                at = pl.ds(s * time_n, time_n)
                xs[0, at, :] = x[s]
                xs[1, at, :] = matmul(back, x[s]).astype(BF16)
                xs[2, pl.ds(s * time_n, span), :] = jnp.zeros((span, width), BF16)
                xs[2, pl.ds(s * time_n + span, time_n - span), :] = x[s, pl.ds(0, time_n - span), :]
                for k in range(3):
                    xt[k, :, at] = xs[k, at, :].T
    x2, y2 = [], []
    c_in = list(sent[3:])
    for j in range(PLANES):
        zj = lax.rem(z + PLANES - j, PLANES)
        x1[j].wait_recv()
        blk = block(zj, py_i, 1 - px_i, core)
        y2.append(pass_on(blk, A, 16 + j, to_y))
        c_in.append(pass_on(blk, ALL, 20 + j, to_c))
        y1[j].wait_recv()
        blk = block(zj, 1 - py_i, px_i, core)
        x2.append(pass_on(blk, B, 24 + j, to_x))
        c_in.append(pass_on(blk, ALL, 28 + j, to_c))
    for j in range(PLANES):
        zj = lax.rem(z + PLANES - j, PLANES)
        y2[j].wait_recv()
        x2[j].wait_recv()
        c_in.append(pass_on(block(zj, 1 - py_i, 1 - px_i, core), ALL, 32 + j, to_c))
    for c in c_in:
        c.wait_recv()

    loads[2].wait()
    for s in range(series_n):
        at = pl.ds(s * time_n, time_n)
        pre = matmul(xs[0, at, :], wide[pl.ds(0, width), :])
        for k in (1, 2):
            pre = pre + matmul(xs[k, at, :], wide[pl.ds(k * width, width), :])
        sig = jax.nn.sigmoid(pre)
        dk[0, at, :] = (cot[s].astype(F32) * (sig * (1.0 + pre * (1.0 - sig)))).astype(BF16)

    c1 = []
    for k in range(3):
        g[pl.ds(k * width, width), :] = matmul(xt[k], dk[0])
        for zz in ((0,), (1,), (2, 3))[k]:
            for q in range(4):
                s1[zz, q] = g[block(zz, q // 2, q % 2, 1 - core), :].astype(BF16)
            c1.append(start(s1.at[zz], r1.at[zz], rs, zz, to_c))

    ahead = jnp.where(column == row + tap, 1.0, 0.0).astype(BF16)

    def grad_input(s):
        total = cot[s].astype(F32)
        first = s * time_n
        dk[1, pl.ds(first, time_n), :] = matmul(ahead, dk[0, pl.ds(first, time_n), :]).astype(BF16)
        dk[2, pl.ds(first, time_n - span), :] = dk[0, pl.ds(first + span, time_n - span), :]
        dk[2, pl.ds(first + time_n - span, span), :] = jnp.zeros((span, width), BF16)
        for k in range(3):
            total = total + matmul_t(dk[k, pl.ds(s * time_n, time_n), :], wide[pl.ds(k * width, width), :])
        gi[s] = total.astype(BF16)
        c = pltpu.make_async_copy(gi.at[s], gi_hbm.at[s], store_sem.at[s])
        c.start()
        return c

    order = (2, 1, 3, 0)
    a2, b2, a3, b3, z4 = {}, {}, {}, {}, {}
    for c in c1:
        c.wait_recv()
    for d in order:
        zz = lax.rem(z + d, PLANES)

        def both(yy, xx, cols):
            return g[block(zz, yy, xx, core), cols] + r1[zz, yy * 2 + xx, :, cols].astype(F32)

        for q in range(2):
            s2a[d, q] = both(q, 1 - px_i, A).astype(BF16)
            s2b[d, q] = both(1 - py_i, q, B).astype(BF16)
        a2[d] = start(s2a.at[d], r2a.at[d], rs, 4 + d, to_x)
        b2[d] = start(s2b.at[d], r2b.at[d], rs, 8 + d, to_y)
    stores = [grad_input(0)]
    for d in order:
        zz = lax.rem(z + d, PLANES)
        a2[d].wait_recv()
        other = 1 - py_i
        s3a[d] = (
            g[block(zz, other, px_i, core), A] + r1[zz, other * 2 + px_i, :, A].astype(F32)
            + r2a[d, other].astype(F32)
        ).astype(BF16)
        a3[d] = start(s3a.at[d], r3a.at[d], rs, 12 + d, to_y)
        b2[d].wait_recv()
        other = 1 - px_i
        s3b[d] = (
            g[block(zz, py_i, other, core), B] + r1[zz, py_i * 2 + other, :, B].astype(F32)
            + r2b[d, other].astype(F32)
        ).astype(BF16)
        b3[d] = start(s3b.at[d], r3b.at[d], rs, 16 + d, to_x)
    stores += [grad_input(s) for s in range(1, series_n)]
    grad = None
    for d in order:
        zz = lax.rem(z + d, PLANES)
        mine = block(zz, py_i, px_i, core)
        q = py_i * 2 + px_i
        a3[d].wait_recv()
        b3[d].wait_recv()
        sum_a = g[mine, A] + r1[zz, q, :, A].astype(F32) + r2a[d, py_i].astype(F32) + r3a[d].astype(F32)
        sum_b = g[mine, B] + r1[zz, q, :, B].astype(F32) + r2b[d, px_i].astype(F32) + r3b[d].astype(F32)
        if d:
            s4[d - 1, :, A] = sum_a.astype(BF16)
            s4[d - 1, :, B] = sum_b.astype(BF16)
            z4[d] = start(s4.at[d - 1], r4.at[d - 1], rs, 19 + d, to_z[d])
        else:
            grad = jnp.concatenate([sum_a, sum_b], 1)
    loads[3].wait()
    loads[4].wait()
    for d in (1, 2, 3):
        z4[d].wait_recv()
        grad = grad + r4[d - 1].astype(F32)
    nw[...], n1[...], n2[...] = adamw(w[...], grad, m1[...], m2[...])
    for i, (src, dst) in enumerate([(nw, nw_hbm), (n1, n1_hbm), (n2, n2_hbm)]):
        c = pltpu.make_async_copy(src, dst, store_sem.at[series_n + i])
        c.start()
        stores.append(c)
    for c in z_copies[1:] + x1 + y1 + x2 + y2 + c_in + c1:
        c.wait_send()
    for group in (a2, b2, a3, b3, z4):
        for c in group.values():
            c.wait_send()
    for c in stores:
        c.wait()


def fused(inputs, cotangent, taps, weight, moment_one, second_moment_state):
    series_n, time_n, width = inputs.shape
    rows = weight.shape[0]
    span = (taps.shape[0] - 1) * DILATION_GAP
    depth = taps.shape[0] * width
    half = width // 2
    flat = series_n * time_n
    state = jax.ShapeDtypeStruct(weight.shape, F32)
    hbm = pl.BlockSpec(memory_space=pl.ANY)
    V = pltpu.VMEM
    return tuple(pl.pallas_call(
        kernel,
        out_shape=[jax.ShapeDtypeStruct(inputs.shape, BF16), state, state, state],
        in_specs=[pl.BlockSpec(memory_space=pltpu.SMEM)] + [hbm] * 5,
        out_specs=[hbm] * 4,
        scratch_shapes=[
            V(inputs.shape, BF16), V(inputs.shape, BF16),
            V(weight.shape, F32), V(weight.shape, F32), V(weight.shape, F32),
            V(inputs.shape, BF16),
            V(weight.shape, F32), V(weight.shape, F32), V(weight.shape, F32),
            V((depth, width), BF16),
            V((3, flat, width), BF16),
            V((3, width, flat), BF16),
            V((3, flat, width), BF16),
            V((depth, width), F32),
            V((PLANES, 4, rows, width), BF16), V((PLANES, 4, rows, width), BF16),
            V((PLANES, 2, rows, half), BF16), V((PLANES, 2, rows, half), BF16),
            V((PLANES, 2, rows, half), BF16), V((PLANES, 2, rows, half), BF16),
            V((PLANES, rows, half), BF16), V((PLANES, rows, half), BF16),
            V((PLANES, rows, half), BF16), V((PLANES, rows, half), BF16),
            V((3, rows, width), BF16), V((3, rows, width), BF16),
            pltpu.SemaphoreType.DMA((5,)), pltpu.SemaphoreType.DMA((series_n + 3,)),
            pltpu.SemaphoreType.DMA((36,)), pltpu.SemaphoreType.DMA((36,)),
            pltpu.SemaphoreType.DMA((23,)), pltpu.SemaphoreType.DMA((23,)),
        ],
        compiler_params=pltpu.CompilerParams(
            collective_id=0, has_side_effects=True, vmem_limit_bytes=48 * 1024 * 1024
        ),
        cost_estimate=pl.CostEstimate(
            flops=6 * flat * depth * width, bytes_accessed=6 * flat * width, transcendentals=flat * width
        ),
    )(taps, inputs, cotangent, weight, moment_one, second_moment_state))


def solution(mesh):
    in_specs = (
        P("series", "tm", None),
        P("series", "tm", None),
        P(),
        P("series", None),
        P("series", None),
        P("series", None),
    )
    out_specs = (P("series", "tm", None), P("series", None), P("series", None), P("series", None))
    step = fused if fits(mesh) else body
    return jax.shard_map(step, mesh=mesh, in_specs=in_specs, out_specs=out_specs, check_vma=False)
```

```python
import functools

import jax
import jax.numpy as jnp
from jax import lax
from jax.experimental import pallas as pl
from jax.experimental.pallas import tpu as pltpu
from jax.sharding import PartitionSpec as P

DILATION_GAP = 64


def passed_along(array, axis, by):
    size = lax.axis_size(axis)
    pairs = [(i, i + by) for i in range(size) if 0 <= i + by < size]
    return lax.ppermute(array, axis, pairs)


def adamw(weight, grad, moment_one, second_moment_state):
    first = 0.9 * moment_one + 0.1 * grad
    second = 0.999 * second_moment_state + 0.001 * grad * grad
    unbiased_one = first / (1.0 - 0.9**10)
    unbiased_two = second / (1.0 - 0.999**10)
    updated = weight - 0.01 * (unbiased_one / (jnp.sqrt(unbiased_two) + 1e-08) + 0.1 * weight)
    return (updated, first, second)


def body(inputs, cotangent, taps, weight, moment_one, second_moment_state):
    series_n, time_n, width = inputs.shape
    tap_count = taps.shape[0]
    receptive_span = (tap_count - 1) * DILATION_GAP
    rows = series_n * time_n
    wide = lax.all_gather(weight.astype(jnp.bfloat16), "series", axis=0, tiled=True)
    earlier = passed_along(inputs[:, time_n - receptive_span :, :], "tm", 1)
    extended = jnp.concatenate([earlier, inputs], 1)
    shifted = [
        lax.dynamic_slice_in_dim(extended, receptive_span - taps[k], time_n, 1)
        for k in range(tap_count)
    ]
    stacked = jnp.concatenate(shifted, 2).reshape(rows, tap_count * width)
    pre = jnp.dot(stacked, wide, preferred_element_type=jnp.float32)
    sig = jax.nn.sigmoid(pre)
    upstream = cotangent.reshape(rows, width)
    dpre_flat = (upstream.astype(jnp.float32) * (sig * (1.0 + pre * (1.0 - sig)))).astype(
        jnp.bfloat16
    )
    dpre = dpre_flat.reshape(series_n, time_n, width)
    ahead = passed_along(dpre[:, :receptive_span, :], "tm", -1)
    later = jnp.concatenate([dpre, ahead], 1)
    result = upstream.astype(jnp.float32)
    for k in range(tap_count):
        moved = lax.dynamic_slice_in_dim(later, taps[k], time_n, 1).reshape(rows, width)
        result = result + lax.dot_general(
            moved,
            wide[k * width : (k + 1) * width],
            (((1,), (1,)), ((), ())),
            preferred_element_type=jnp.float32,
        )
    grad_input = result.astype(jnp.bfloat16).reshape(series_n, time_n, width)
    grad_shard = lax.psum_scatter(
        lax.dot_general(
            stacked, dpre_flat, (((0,), (0,)), ((), ())), preferred_element_type=jnp.float32
        ),
        "series",
        scatter_dimension=0,
        tiled=True,
    )
    grad_shard = lax.psum(grad_shard, "tm")
    new_weight, new_moment_one, new_moment_two = adamw(
        weight, grad_shard, moment_one, second_moment_state
    )
    return (grad_input, new_weight, new_moment_one, new_moment_two)


MESH = pl.DeviceIdType.MESH
F32, BF16 = jnp.float32, jnp.bfloat16
PLANES, IN_PLANE = 4, 8


def fits(mesh):
    return mesh.shape["tm"] == 1 and mesh.shape["series"] == PLANES * IN_PLANE


def matmul(a, b):
    return jnp.dot(a, b, preferred_element_type=F32)


def matmul_t(a, b):
    return lax.dot_general(a, b, (((1,), (1,)), ((), ())), preferred_element_type=F32)


def kernel(
    taps_ref, x_hbm, cot_hbm, w_hbm, gi_hbm, grad_hbm,
    x, cot, w, gi, grad_ref,
    wide, xs, xt, pre, dk, g, s1, r1, s2a, s2b, r2a, r2b, s3a, s3b, r3a, r3b, s4, r4,
    load_sem, store_sem, ag_send, ag_recv, rs_send, rs_recv,
):
    series_n, time_n, width = x.shape
    flat = series_n * time_n
    span = 2 * DILATION_GAP
    rows = w.shape[0]
    group = IN_PLANE * rows
    half = width // 2
    tm = lax.axis_index("tm")
    me = lax.axis_index("series")
    core = lax.rem(me, 2)
    px = lax.rem(me // 2, 2)
    py = lax.rem(me // 4, 2)
    z = me // IN_PLANE

    def index(zz, yy, xx, cc):
        return ((zz * 2 + yy) * 2 + xx) * 2 + cc

    def block(zz, yy, xx, cc):
        return pl.ds(pl.multiple_of(index(zz, yy, xx, cc) * rows, 16), rows)

    to_x = (tm, index(z, py, 1 - px, core))
    to_y = (tm, index(z, 1 - py, px, core))
    to_c = (tm, index(z, py, px, 1 - core))
    to_z = [None] + [(tm, index(lax.rem(z + d, PLANES), py, px, core)) for d in (1, 2, 3)]

    loads = [
        pltpu.make_async_copy(src, dst, load_sem.at[i])
        for i, (src, dst) in enumerate([(w_hbm, w), (x_hbm, x), (cot_hbm, cot)])
    ]
    for c in loads:
        c.start()

    barrier = pltpu.get_barrier_semaphore()
    for dev in (to_x, to_y, to_c, *to_z[1:]):
        pl.semaphore_signal(barrier, inc=1, device_id=dev, device_id_type=MESH)

    loads[0].wait()
    own = block(z, py, px, core)
    wide[own, :] = w[...].astype(BF16)

    tap = taps_ref[1]
    row = lax.broadcasted_iota(jnp.int32, (time_n, time_n), 0)
    column = lax.broadcasted_iota(jnp.int32, (time_n, time_n), 1)
    back = jnp.where(column == row - tap, 1.0, 0.0).astype(BF16)
    ahead = jnp.where(column == row + tap, 1.0, 0.0).astype(BF16)
    taps_at = [pl.ds(k * width, width) for k in range(3)]

    def shift(s):
        first = s * time_n
        at = pl.ds(first, time_n)
        xs[at, taps_at[0]] = x[s]
        xs[at, taps_at[1]] = matmul(back, x[s]).astype(BF16)
        xs[pl.ds(first, span), taps_at[2]] = jnp.zeros((span, width), BF16)
        xs[pl.ds(first + span, time_n - span), taps_at[2]] = x[s, pl.ds(0, time_n - span), :]

    def transpose(s):
        first = s * time_n
        at = pl.ds(first, time_n)
        turned = x[s].T
        xt[taps_at[0], at] = turned
        xt[taps_at[1], at] = matmul(turned, ahead).astype(BF16)
        xt[taps_at[2], pl.ds(first, span)] = jnp.zeros((width, span), BF16)
        xt[taps_at[2], pl.ds(first + span, time_n - span)] = turned[:, : time_n - span]

    loads[1].wait()
    shift(0)
    pl.semaphore_wait(barrier, 6)

    def start(src, dst, sems, k, dev):
        c = pltpu.make_async_remote_copy(
            src_ref=src, dst_ref=dst, send_sem=sems[0].at[k], recv_sem=sems[1].at[k],
            device_id=dev, device_id_type=MESH,
        )
        c.start()
        return c

    ag = (ag_send, ag_recv)
    rs = (rs_send, rs_recv)
    A, B, ALL = pl.ds(0, half), pl.ds(half, half), pl.ds(0, width)

    def pass_on(blk, cols, k, dev):
        return start(wide.at[blk, cols], wide.at[blk, cols], ag, k, dev)

    def before(j):
        return lax.rem(z + PLANES - j, PLANES)

    z_in = [None] + [pass_on(own, ALL, d, to_z[d]) for d in (1, 2, 3)]
    x1, y1, x2, y2, c_in = [], [], [], [], [[], [], [], []]

    def first_hop(j):
        if j:
            z_in[j].wait_recv()
        blk = block(before(j), py, px, core)
        x1.append(pass_on(blk, ALL, 4 + j, to_x))
        y1.append(pass_on(blk, ALL, 8 + j, to_y))
        c_in[j].append(pass_on(blk, ALL, 12 + j, to_c))

    def second_hop(j):
        x1[j].wait_recv()
        blk = block(before(j), py, 1 - px, core)
        y2.append(pass_on(blk, A, 16 + j, to_y))
        c_in[j].append(pass_on(blk, ALL, 20 + j, to_c))
        y1[j].wait_recv()
        blk = block(before(j), 1 - py, px, core)
        x2.append(pass_on(blk, B, 24 + j, to_x))
        c_in[j].append(pass_on(blk, ALL, 28 + j, to_c))

    def last_hop(j):
        y2[j].wait_recv()
        x2[j].wait_recv()
        c_in[j].append(pass_on(block(before(j), 1 - py, 1 - px, core), ALL, 32 + j, to_c))

    def forward(j):
        for c in c_in[j]:
            c.wait_recv()
        at = pl.ds(pl.multiple_of(before(j) * group, 128), group)
        term = matmul(xs[:, at], wide[at, :])
        pre[...] = term if j == 0 else pre[...] + term

    first_hop(0)
    shift(1)
    first_hop(1)
    second_hop(0)
    transpose(0)
    first_hop(2)
    second_hop(1)
    last_hop(0)
    transpose(1)
    first_hop(3)
    second_hop(2)
    last_hop(1)
    forward(0)
    second_hop(3)
    last_hop(2)
    forward(1)
    last_hop(3)
    forward(2)
    loads[2].wait()
    for c in c_in[3]:
        c.wait_recv()
    at = pl.ds(pl.multiple_of(before(3) * group, 128), group)
    for s in range(series_n):
        part = pl.ds(s * time_n, time_n)
        total = pre[part, :] + matmul(xs[part, at], wide[at, :])
        sig = jax.nn.sigmoid(total)
        dk[0, part, :] = (cot[s].astype(F32) * (sig * (1.0 + total * (1.0 - sig)))).astype(BF16)

    c1, a2, b2, a3, b3, z4 = {}, {}, {}, {}, {}, {}

    def after(d):
        return lax.rem(z + d, PLANES)

    def weight_grad(d):
        zz = after(d)
        at = pl.ds(pl.multiple_of(zz * group, 128), group)
        g[at, :] = matmul(xt[at, :], dk[0])
        for q in range(4):
            s1[d, q] = g[block(zz, q // 2, q % 2, 1 - core), :].astype(BF16)
        c1[d] = start(s1.at[d], r1.at[d], rs, d, to_c)

    def both(d, yy, xx, cols):
        return g[block(after(d), yy, xx, core), cols] + r1[d, yy * 2 + xx, :, cols].astype(F32)

    def reduce_one(d):
        c1[d].wait_recv()
        for q in range(2):
            s2a[d, q] = both(d, q, 1 - px, A).astype(BF16)
            s2b[d, q] = both(d, 1 - py, q, B).astype(BF16)
        a2[d] = start(s2a.at[d], r2a.at[d], rs, 4 + d, to_x)
        b2[d] = start(s2b.at[d], r2b.at[d], rs, 8 + d, to_y)

    def reduce_two(d):
        a2[d].wait_recv()
        s3a[d] = (both(d, 1 - py, px, A) + r2a[d, 1 - py].astype(F32)).astype(BF16)
        a3[d] = start(s3a.at[d], r3a.at[d], rs, 12 + d, to_y)
        b2[d].wait_recv()
        s3b[d] = (both(d, py, 1 - px, B) + r2b[d, 1 - px].astype(F32)).astype(BF16)
        b3[d] = start(s3b.at[d], r3b.at[d], rs, 16 + d, to_x)

    def reduce_three(d):
        a3[d].wait_recv()
        b3[d].wait_recv()
        sum_a = both(d, py, px, A) + r2a[d, py].astype(F32) + r3a[d].astype(F32)
        sum_b = both(d, py, px, B) + r2b[d, px].astype(F32) + r3b[d].astype(F32)
        if d:
            s4[d - 1, :, A] = sum_a.astype(BF16)
            s4[d - 1, :, B] = sum_b.astype(BF16)
            z4[d] = start(s4.at[d - 1], r4.at[d - 1], rs, 19 + d, to_z[d])
        else:
            grad_ref[:, A] = sum_a
            grad_ref[:, B] = sum_b

    stores = []

    def shift_dpre(s):
        first = s * time_n
        dk[1, pl.ds(first, time_n), :] = matmul(ahead, dk[0, pl.ds(first, time_n), :]).astype(BF16)
        dk[2, pl.ds(first, time_n - span), :] = dk[0, pl.ds(first + span, time_n - span), :]
        dk[2, pl.ds(first + time_n - span, span), :] = jnp.zeros((span, width), BF16)

    def grad_input(s):
        total = cot[s].astype(F32)
        for k in range(3):
            total = total + matmul_t(dk[k, pl.ds(s * time_n, time_n), :], wide[taps_at[k], :])
        gi[s] = total.astype(BF16)
        c = pltpu.make_async_copy(gi.at[s], gi_hbm.at[s], store_sem.at[s])
        c.start()
        stores.append(c)

    o = (2, 1, 3, 0)
    weight_grad(o[0])
    weight_grad(o[1])
    reduce_one(o[0])
    weight_grad(o[2])
    reduce_one(o[1])
    weight_grad(o[3])
    reduce_one(o[2])
    shift_dpre(0)
    reduce_one(o[3])
    reduce_two(o[0])
    shift_dpre(1)
    reduce_two(o[1])
    grad_input(0)
    reduce_two(o[2])
    reduce_three(o[0])
    reduce_two(o[3])
    reduce_three(o[1])
    grad_input(1)
    reduce_three(o[2])
    reduce_three(o[3])
    total = grad_ref[...]
    for d in (2, 1, 3):
        z4[d].wait_recv()
        total = total + r4[d - 1].astype(F32)
    grad_ref[...] = total
    c = pltpu.make_async_copy(grad_ref, grad_hbm, store_sem.at[series_n])
    c.start()
    stores.append(c)
    for c in z_in[1:] + x1 + y1 + x2 + y2 + sum(c_in, []):
        c.wait_send()
    for made in (c1, a2, b2, a3, b3, z4):
        for c in made.values():
            c.wait_send()
    for c in stores:
        c.wait()


def finish(gi, grad, weight, moment_one, second_moment_state, gi_out, nw, n1, n2, sems):
    copies = [pltpu.make_async_copy(gi.at[s], gi_out.at[s], sems.at[s]) for s in range(gi.shape[0])]
    for c in copies:
        c.start()
    nw[...], n1[...], n2[...] = adamw(weight[...], grad[...], moment_one[...], second_moment_state[...])
    for c in copies:
        c.wait()


def fused(inputs, cotangent, taps, weight, moment_one, second_moment_state):
    series_n, time_n, width = inputs.shape
    rows = weight.shape[0]
    depth = taps.shape[0] * width
    half = width // 2
    flat = series_n * time_n
    state = jax.ShapeDtypeStruct(weight.shape, F32)
    hbm = pl.BlockSpec(memory_space=pltpu.HBM)
    vmem = pl.BlockSpec(memory_space=pltpu.VMEM)
    V = pltpu.VMEM
    gi, grad = pl.pallas_call(
        kernel,
        out_shape=[jax.ShapeDtypeStruct(inputs.shape, BF16), state],
        in_specs=[pl.BlockSpec(memory_space=pltpu.SMEM)] + [hbm] * 3,
        out_specs=[hbm] * 2,
        scratch_shapes=[
            V(inputs.shape, BF16), V(inputs.shape, BF16), V(weight.shape, F32),
            V(inputs.shape, BF16), V(weight.shape, F32),
            V((depth, width), BF16),
            V((flat, depth), BF16),
            V((depth, flat), BF16),
            V((flat, width), F32),
            V((3, flat, width), BF16),
            V((depth, width), F32),
            V((PLANES, 4, rows, width), BF16), V((PLANES, 4, rows, width), BF16),
            V((PLANES, 2, rows, half), BF16), V((PLANES, 2, rows, half), BF16),
            V((PLANES, 2, rows, half), BF16), V((PLANES, 2, rows, half), BF16),
            V((PLANES, rows, half), BF16), V((PLANES, rows, half), BF16),
            V((PLANES, rows, half), BF16), V((PLANES, rows, half), BF16),
            V((3, rows, width), BF16), V((3, rows, width), BF16),
            pltpu.SemaphoreType.DMA((3,)), pltpu.SemaphoreType.DMA((series_n + 1,)),
            pltpu.SemaphoreType.DMA((36,)), pltpu.SemaphoreType.DMA((36,)),
            pltpu.SemaphoreType.DMA((23,)), pltpu.SemaphoreType.DMA((23,)),
        ],
        compiler_params=pltpu.CompilerParams(
            collective_id=0, has_side_effects=True, vmem_limit_bytes=63 * 1024 * 1024
        ),
        cost_estimate=pl.CostEstimate(
            flops=6 * flat * depth * width, bytes_accessed=6 * flat * width, transcendentals=flat * width
        ),
    )(taps, inputs, cotangent, weight)
    return tuple(pl.pallas_call(
        finish,
        out_shape=[jax.ShapeDtypeStruct(inputs.shape, BF16), state, state, state],
        in_specs=[hbm] + [vmem] * 4,
        out_specs=[hbm] + [vmem] * 3,
        scratch_shapes=[pltpu.SemaphoreType.DMA((series_n,))],
        compiler_params=pltpu.CompilerParams(vmem_limit_bytes=65024 * 1024),
        cost_estimate=pl.CostEstimate(flops=20 * rows * width, bytes_accessed=28 * rows * width, transcendentals=0),
    )(gi, grad, weight, moment_one, second_moment_state))


def solution(mesh):
    in_specs = (
        P("series", "tm", None),
        P("series", "tm", None),
        P(),
        P("series", None),
        P("series", None),
        P("series", None),
    )
    out_specs = (P("series", "tm", None), P("series", None), P("series", None), P("series", None))
    step = fused if fits(mesh) else body
    return jax.shard_map(step, mesh=mesh, in_specs=in_specs, out_specs=out_specs, check_vma=False)
```

```python
import functools

import jax
import jax.numpy as jnp
from jax import lax
from jax.experimental import pallas as pl
from jax.experimental.pallas import tpu as pltpu
from jax.sharding import PartitionSpec as P

DILATION_GAP = 64


def passed_along(array, axis, by):
    size = lax.axis_size(axis)
    pairs = [(i, i + by) for i in range(size) if 0 <= i + by < size]
    return lax.ppermute(array, axis, pairs)


def adamw(weight, grad, moment_one, second_moment_state):
    first = 0.9 * moment_one + 0.1 * grad
    second = 0.999 * second_moment_state + 0.001 * grad * grad
    unbiased_one = first / (1.0 - 0.9**10)
    unbiased_two = second / (1.0 - 0.999**10)
    updated = weight - 0.01 * (unbiased_one / (jnp.sqrt(unbiased_two) + 1e-08) + 0.1 * weight)
    return (updated, first, second)


def body(inputs, cotangent, taps, weight, moment_one, second_moment_state):
    series_n, time_n, width = inputs.shape
    tap_count = taps.shape[0]
    receptive_span = (tap_count - 1) * DILATION_GAP
    rows = series_n * time_n
    wide = lax.all_gather(weight.astype(jnp.bfloat16), "series", axis=0, tiled=True)
    earlier = passed_along(inputs[:, time_n - receptive_span :, :], "tm", 1)
    extended = jnp.concatenate([earlier, inputs], 1)
    shifted = [
        lax.dynamic_slice_in_dim(extended, receptive_span - taps[k], time_n, 1)
        for k in range(tap_count)
    ]
    stacked = jnp.concatenate(shifted, 2).reshape(rows, tap_count * width)
    pre = jnp.dot(stacked, wide, preferred_element_type=jnp.float32)
    sig = jax.nn.sigmoid(pre)
    upstream = cotangent.reshape(rows, width)
    dpre_flat = (upstream.astype(jnp.float32) * (sig * (1.0 + pre * (1.0 - sig)))).astype(
        jnp.bfloat16
    )
    dpre = dpre_flat.reshape(series_n, time_n, width)
    ahead = passed_along(dpre[:, :receptive_span, :], "tm", -1)
    later = jnp.concatenate([dpre, ahead], 1)
    result = upstream.astype(jnp.float32)
    for k in range(tap_count):
        moved = lax.dynamic_slice_in_dim(later, taps[k], time_n, 1).reshape(rows, width)
        result = result + lax.dot_general(
            moved,
            wide[k * width : (k + 1) * width],
            (((1,), (1,)), ((), ())),
            preferred_element_type=jnp.float32,
        )
    grad_input = result.astype(jnp.bfloat16).reshape(series_n, time_n, width)
    grad_shard = lax.psum_scatter(
        lax.dot_general(
            stacked, dpre_flat, (((0,), (0,)), ((), ())), preferred_element_type=jnp.float32
        ),
        "series",
        scatter_dimension=0,
        tiled=True,
    )
    grad_shard = lax.psum(grad_shard, "tm")
    new_weight, new_moment_one, new_moment_two = adamw(
        weight, grad_shard, moment_one, second_moment_state
    )
    return (grad_input, new_weight, new_moment_one, new_moment_two)


MESH = pl.DeviceIdType.MESH
F32, BF16 = jnp.float32, jnp.bfloat16
PLANES, IN_PLANE = 4, 8


def fits(mesh):
    return mesh.shape["tm"] == 1 and mesh.shape["series"] == PLANES * IN_PLANE


def matmul(a, b):
    return jnp.dot(a, b, preferred_element_type=F32)


def matmul_t(a, b):
    return lax.dot_general(a, b, (((1,), (1,)), ((), ())), preferred_element_type=F32)


def kernel(
    taps_ref, x_hbm, cot_hbm, w_hbm, gi_hbm, grad_hbm,
    x, cot, w, gi, grad_ref,
    wide, xs, xt, pre, dk, g, s1, r1, s2a, s2b, r2a, r2b, s3a, s3b, r3a, r3b, s4, r4,
    load_sem, store_sem, ag_send, ag_recv, rs_send, rs_recv,
):
    series_n, time_n, width = x.shape
    flat = series_n * time_n
    span = 2 * DILATION_GAP
    rows = w.shape[0]
    group = IN_PLANE * rows
    half = width // 2
    tm = lax.axis_index("tm")
    me = lax.axis_index("series")
    core = lax.rem(me, 2)
    px = lax.rem(me // 2, 2)
    py = lax.rem(me // 4, 2)
    z = me // IN_PLANE

    def index(zz, yy, xx, cc):
        return ((zz * 2 + yy) * 2 + xx) * 2 + cc

    def block(zz, yy, xx, cc):
        return pl.ds(pl.multiple_of(index(zz, yy, xx, cc) * rows, 16), rows)

    to_x = (tm, index(z, py, 1 - px, core))
    to_y = (tm, index(z, 1 - py, px, core))
    to_c = (tm, index(z, py, px, 1 - core))
    to_z = [None] + [(tm, index(lax.rem(z + d, PLANES), py, px, core)) for d in (1, 2, 3)]

    loads = [
        pltpu.make_async_copy(src, dst, load_sem.at[i])
        for i, (src, dst) in enumerate([(w_hbm, w), (x_hbm, x), (cot_hbm, cot)])
    ]
    for c in loads:
        c.start()

    barrier = pltpu.get_barrier_semaphore()
    for dev in (to_x, to_y, to_c, *to_z[1:]):
        pl.semaphore_signal(barrier, inc=1, device_id=dev, device_id_type=MESH)

    loads[0].wait()
    own = block(z, py, px, core)
    wide[own, :] = w[...].astype(BF16)

    tap = taps_ref[1]
    row = lax.broadcasted_iota(jnp.int32, (time_n, time_n), 0)
    column = lax.broadcasted_iota(jnp.int32, (time_n, time_n), 1)
    back = jnp.where(column == row - tap, 1.0, 0.0).astype(BF16)
    ahead = jnp.where(column == row + tap, 1.0, 0.0).astype(BF16)
    taps_at = [pl.ds(k * width, width) for k in range(3)]

    def shift(s):
        first = s * time_n
        at = pl.ds(first, time_n)
        xs[at, taps_at[0]] = x[s]
        xs[at, taps_at[1]] = matmul(back, x[s]).astype(BF16)
        xs[pl.ds(first, span), taps_at[2]] = jnp.zeros((span, width), BF16)
        xs[pl.ds(first + span, time_n - span), taps_at[2]] = x[s, pl.ds(0, time_n - span), :]

    def transpose(s):
        first = s * time_n
        at = pl.ds(first, time_n)
        turned = x[s].T
        xt[taps_at[0], at] = turned
        xt[taps_at[1], at] = matmul(turned, ahead).astype(BF16)
        xt[taps_at[2], pl.ds(first, span)] = jnp.zeros((width, span), BF16)
        xt[taps_at[2], pl.ds(first + span, time_n - span)] = turned[:, : time_n - span]

    loads[1].wait()
    shift(0)
    pl.semaphore_wait(barrier, 6)

    def start(src, dst, sems, k, dev):
        c = pltpu.make_async_remote_copy(
            src_ref=src, dst_ref=dst, send_sem=sems[0].at[k], recv_sem=sems[1].at[k],
            device_id=dev, device_id_type=MESH,
        )
        c.start()
        return c

    ag = (ag_send, ag_recv)
    rs = (rs_send, rs_recv)
    A, B, ALL = pl.ds(0, half), pl.ds(half, half), pl.ds(0, width)

    def pass_on(blk, cols, k, dev):
        return start(wide.at[blk, cols], wide.at[blk, cols], ag, k, dev)

    def before(j):
        return lax.rem(z + PLANES - j, PLANES)

    z_in = [None] + [pass_on(own, ALL, d, to_z[d]) for d in (1, 2, 3)]
    x1, y1, x2, y2, c_in = [], [], [], [], [[], [], [], []]

    def first_hop(j):
        if j:
            z_in[j].wait_recv()
        blk = block(before(j), py, px, core)
        x1.append(pass_on(blk, ALL, 4 + j, to_x))
        y1.append(pass_on(blk, ALL, 8 + j, to_y))
        c_in[j].append(pass_on(blk, ALL, 12 + j, to_c))

    def second_hop(j):
        x1[j].wait_recv()
        blk = block(before(j), py, 1 - px, core)
        y2.append(pass_on(blk, A, 16 + j, to_y))
        c_in[j].append(pass_on(blk, ALL, 20 + j, to_c))
        y1[j].wait_recv()
        blk = block(before(j), 1 - py, px, core)
        x2.append(pass_on(blk, B, 24 + j, to_x))
        c_in[j].append(pass_on(blk, ALL, 28 + j, to_c))

    def last_hop(j):
        y2[j].wait_recv()
        x2[j].wait_recv()
        c_in[j].append(pass_on(block(before(j), 1 - py, 1 - px, core), ALL, 32 + j, to_c))

    def forward(j):
        for c in c_in[j]:
            c.wait_recv()
        at = pl.ds(pl.multiple_of(before(j) * group, 128), group)
        term = matmul(xs[:, at], wide[at, :])
        pre[...] = term if j == 0 else pre[...] + term

    first_hop(0)
    shift(1)
    first_hop(1)
    second_hop(0)
    transpose(0)
    first_hop(2)
    second_hop(1)
    last_hop(0)
    transpose(1)
    first_hop(3)
    second_hop(2)
    last_hop(1)
    forward(0)
    second_hop(3)
    last_hop(2)
    forward(1)
    last_hop(3)
    forward(2)
    loads[2].wait()
    for c in c_in[3]:
        c.wait_recv()
    at = pl.ds(pl.multiple_of(before(3) * group, 128), group)
    for s in range(series_n):
        part = pl.ds(s * time_n, time_n)
        total = pre[part, :] + matmul(xs[part, at], wide[at, :])
        sig = jax.nn.sigmoid(total)
        dk[0, part, :] = (cot[s].astype(F32) * (sig * (1.0 + total * (1.0 - sig)))).astype(BF16)

    c1, a2, b2, a3, b3, z4 = {}, {}, {}, {}, {}, {}

    def after(d):
        return lax.rem(z + d, PLANES)

    def weight_grad(d):
        zz = after(d)
        at = pl.ds(pl.multiple_of(zz * group, 128), group)
        g[at, :] = matmul(xt[at, :], dk[0])
        for q in range(4):
            s1[d, q] = g[block(zz, q // 2, q % 2, 1 - core), :].astype(BF16)
        c1[d] = start(s1.at[d], r1.at[d], rs, d, to_c)

    def both(d, yy, xx, cols):
        return g[block(after(d), yy, xx, core), cols] + r1[d, yy * 2 + xx, :, cols].astype(F32)

    def reduce_one(d):
        c1[d].wait_recv()
        for q in range(2):
            s2a[d, q] = both(d, q, 1 - px, A).astype(BF16)
            s2b[d, q] = both(d, 1 - py, q, B).astype(BF16)
        a2[d] = start(s2a.at[d], r2a.at[d], rs, 4 + d, to_x)
        b2[d] = start(s2b.at[d], r2b.at[d], rs, 8 + d, to_y)

    def reduce_two(d):
        a2[d].wait_recv()
        s3a[d] = (both(d, 1 - py, px, A) + r2a[d, 1 - py].astype(F32)).astype(BF16)
        a3[d] = start(s3a.at[d], r3a.at[d], rs, 12 + d, to_y)
        b2[d].wait_recv()
        s3b[d] = (both(d, py, 1 - px, B) + r2b[d, 1 - px].astype(F32)).astype(BF16)
        b3[d] = start(s3b.at[d], r3b.at[d], rs, 16 + d, to_x)

    def reduce_three(d):
        a3[d].wait_recv()
        b3[d].wait_recv()
        sum_a = both(d, py, px, A) + r2a[d, py].astype(F32) + r3a[d].astype(F32)
        sum_b = both(d, py, px, B) + r2b[d, px].astype(F32) + r3b[d].astype(F32)
        if d:
            s4[d - 1, :, A] = sum_a.astype(BF16)
            s4[d - 1, :, B] = sum_b.astype(BF16)
            z4[d] = start(s4.at[d - 1], r4.at[d - 1], rs, 19 + d, to_z[d])
        else:
            grad_ref[:, A] = sum_a
            grad_ref[:, B] = sum_b

    stores = []

    def shift_dpre(s):
        first = s * time_n
        dk[1, pl.ds(first, time_n), :] = matmul(ahead, dk[0, pl.ds(first, time_n), :]).astype(BF16)
        dk[2, pl.ds(first, time_n - span), :] = dk[0, pl.ds(first + span, time_n - span), :]
        dk[2, pl.ds(first + time_n - span, span), :] = jnp.zeros((span, width), BF16)

    def grad_input(s):
        total = cot[s].astype(F32)
        for k in range(3):
            total = total + matmul_t(dk[k, pl.ds(s * time_n, time_n), :], wide[taps_at[k], :])
        gi[s] = total.astype(BF16)
        c = pltpu.make_async_copy(gi.at[s], gi_hbm.at[s], store_sem.at[s])
        c.start()
        stores.append(c)

    o = (2, 1, 3, 0)
    weight_grad(o[0])
    weight_grad(o[1])
    reduce_one(o[0])
    weight_grad(o[2])
    reduce_one(o[1])
    weight_grad(o[3])
    reduce_one(o[2])
    shift_dpre(0)
    reduce_one(o[3])
    reduce_two(o[0])
    shift_dpre(1)
    reduce_two(o[1])
    grad_input(0)
    reduce_two(o[2])
    reduce_three(o[0])
    reduce_two(o[3])
    reduce_three(o[1])
    grad_input(1)
    reduce_three(o[2])
    reduce_three(o[3])
    total = grad_ref[...]
    for d in (2, 1, 3):
        z4[d].wait_recv()
        total = total + r4[d - 1].astype(F32)
    grad_ref[...] = total
    c = pltpu.make_async_copy(grad_ref, grad_hbm, store_sem.at[series_n])
    c.start()
    stores.append(c)
    for c in z_in[1:] + x1 + y1 + x2 + y2 + sum(c_in, []):
        c.wait_send()
    for made in (c1, a2, b2, a3, b3, z4):
        for c in made.values():
            c.wait_send()
    for c in stores:
        c.wait()


def finish(
    gi, grad, weight, moment_one, second_moment_state, gi_out, nw_out, n1_out, n2_out,
    held, state, new, in_sem, out_sem, state_sem, new_sem,
):
    parts = [(s, pl.ds(h * held.shape[1] // 2, held.shape[1] // 2)) for s in range(held.shape[0]) for h in range(2)]
    inward = [pltpu.make_async_copy(gi.at[p], held.at[p], in_sem.at[i]) for i, p in enumerate(parts)]
    states = [
        pltpu.make_async_copy(src, state.at[i], state_sem.at[i])
        for i, src in enumerate((weight, grad, moment_one, second_moment_state))
    ]
    for c in inward + states:
        c.start()
    outward = []
    for i, p in enumerate(parts):
        inward[i].wait()
        outward.append(pltpu.make_async_copy(held.at[p], gi_out.at[p], out_sem.at[i]))
        outward[-1].start()
    for c in states:
        c.wait()
    new[0], new[1], new[2] = adamw(state[0], state[1], state[2], state[3])
    for i, dst in enumerate((nw_out, n1_out, n2_out)):
        outward.append(pltpu.make_async_copy(new.at[i], dst, new_sem.at[i]))
        outward[-1].start()
    for c in outward:
        c.wait()


def fused(inputs, cotangent, taps, weight, moment_one, second_moment_state):
    series_n, time_n, width = inputs.shape
    rows = weight.shape[0]
    depth = taps.shape[0] * width
    half = width // 2
    flat = series_n * time_n
    state = jax.ShapeDtypeStruct(weight.shape, F32)
    hbm = pl.BlockSpec(memory_space=pltpu.HBM)
    V = pltpu.VMEM
    gi, grad = pl.pallas_call(
        kernel,
        out_shape=[jax.ShapeDtypeStruct(inputs.shape, BF16), state],
        in_specs=[pl.BlockSpec(memory_space=pltpu.SMEM)] + [hbm] * 3,
        out_specs=[hbm] * 2,
        scratch_shapes=[
            V(inputs.shape, BF16), V(inputs.shape, BF16), V(weight.shape, F32),
            V(inputs.shape, BF16), V(weight.shape, F32),
            V((depth, width), BF16),
            V((flat, depth), BF16),
            V((depth, flat), BF16),
            V((flat, width), F32),
            V((3, flat, width), BF16),
            V((depth, width), F32),
            V((PLANES, 4, rows, width), BF16), V((PLANES, 4, rows, width), BF16),
            V((PLANES, 2, rows, half), BF16), V((PLANES, 2, rows, half), BF16),
            V((PLANES, 2, rows, half), BF16), V((PLANES, 2, rows, half), BF16),
            V((PLANES, rows, half), BF16), V((PLANES, rows, half), BF16),
            V((PLANES, rows, half), BF16), V((PLANES, rows, half), BF16),
            V((3, rows, width), BF16), V((3, rows, width), BF16),
            pltpu.SemaphoreType.DMA((3,)), pltpu.SemaphoreType.DMA((series_n + 1,)),
            pltpu.SemaphoreType.DMA((36,)), pltpu.SemaphoreType.DMA((36,)),
            pltpu.SemaphoreType.DMA((23,)), pltpu.SemaphoreType.DMA((23,)),
        ],
        compiler_params=pltpu.CompilerParams(
            collective_id=0, has_side_effects=True, vmem_limit_bytes=63 * 1024 * 1024
        ),
        cost_estimate=pl.CostEstimate(
            flops=6 * flat * depth * width, bytes_accessed=6 * flat * width, transcendentals=flat * width
        ),
    )(taps, inputs, cotangent, weight)
    return tuple(pl.pallas_call(
        finish,
        out_shape=[jax.ShapeDtypeStruct(inputs.shape, BF16), state, state, state],
        in_specs=[hbm] * 5,
        out_specs=[hbm] * 4,
        scratch_shapes=[
            V(inputs.shape, BF16), V((4, rows, width), F32), V((3, rows, width), F32),
            pltpu.SemaphoreType.DMA((2 * series_n,)), pltpu.SemaphoreType.DMA((2 * series_n,)),
            pltpu.SemaphoreType.DMA((4,)), pltpu.SemaphoreType.DMA((3,)),
        ],
        compiler_params=pltpu.CompilerParams(vmem_limit_bytes=63 * 1024 * 1024),
        cost_estimate=pl.CostEstimate(flops=20 * rows * width, bytes_accessed=28 * rows * width, transcendentals=0),
    )(gi, grad, weight, moment_one, second_moment_state))


def solution(mesh):
    in_specs = (
        P("series", "tm", None),
        P("series", "tm", None),
        P(),
        P("series", None),
        P("series", None),
        P("series", None),
    )
    out_specs = (P("series", "tm", None), P("series", None), P("series", None), P("series", None))
    step = fused if fits(mesh) else body
    return jax.shard_map(step, mesh=mesh, in_specs=in_specs, out_specs=out_specs, check_vma=False)
```

```python
import functools

import jax
import jax.numpy as jnp
from jax import lax
from jax.experimental import pallas as pl
from jax.experimental.pallas import tpu as pltpu
from jax.sharding import PartitionSpec as P

DILATION_GAP = 64


def passed_along(array, axis, by):
    size = lax.axis_size(axis)
    pairs = [(i, i + by) for i in range(size) if 0 <= i + by < size]
    return lax.ppermute(array, axis, pairs)


def adamw(weight, grad, moment_one, second_moment_state):
    first = 0.9 * moment_one + 0.1 * grad
    second = 0.999 * second_moment_state + 0.001 * grad * grad
    unbiased_one = first / (1.0 - 0.9**10)
    unbiased_two = second / (1.0 - 0.999**10)
    updated = weight - 0.01 * (unbiased_one / (jnp.sqrt(unbiased_two) + 1e-08) + 0.1 * weight)
    return (updated, first, second)


def body(inputs, cotangent, taps, weight, moment_one, second_moment_state):
    series_n, time_n, width = inputs.shape
    tap_count = taps.shape[0]
    receptive_span = (tap_count - 1) * DILATION_GAP
    rows = series_n * time_n
    wide = lax.all_gather(weight.astype(jnp.bfloat16), "series", axis=0, tiled=True)
    earlier = passed_along(inputs[:, time_n - receptive_span :, :], "tm", 1)
    extended = jnp.concatenate([earlier, inputs], 1)
    shifted = [
        lax.dynamic_slice_in_dim(extended, receptive_span - taps[k], time_n, 1)
        for k in range(tap_count)
    ]
    stacked = jnp.concatenate(shifted, 2).reshape(rows, tap_count * width)
    pre = jnp.dot(stacked, wide, preferred_element_type=jnp.float32)
    sig = jax.nn.sigmoid(pre)
    upstream = cotangent.reshape(rows, width)
    dpre_flat = (upstream.astype(jnp.float32) * (sig * (1.0 + pre * (1.0 - sig)))).astype(
        jnp.bfloat16
    )
    dpre = dpre_flat.reshape(series_n, time_n, width)
    ahead = passed_along(dpre[:, :receptive_span, :], "tm", -1)
    later = jnp.concatenate([dpre, ahead], 1)
    result = upstream.astype(jnp.float32)
    for k in range(tap_count):
        moved = lax.dynamic_slice_in_dim(later, taps[k], time_n, 1).reshape(rows, width)
        result = result + lax.dot_general(
            moved,
            wide[k * width : (k + 1) * width],
            (((1,), (1,)), ((), ())),
            preferred_element_type=jnp.float32,
        )
    grad_input = result.astype(jnp.bfloat16).reshape(series_n, time_n, width)
    grad_shard = lax.psum_scatter(
        lax.dot_general(
            stacked, dpre_flat, (((0,), (0,)), ((), ())), preferred_element_type=jnp.float32
        ),
        "series",
        scatter_dimension=0,
        tiled=True,
    )
    grad_shard = lax.psum(grad_shard, "tm")
    new_weight, new_moment_one, new_moment_two = adamw(
        weight, grad_shard, moment_one, second_moment_state
    )
    return (grad_input, new_weight, new_moment_one, new_moment_two)


MESH = pl.DeviceIdType.MESH
F32, BF16 = jnp.float32, jnp.bfloat16
PLANES, IN_PLANE = 4, 8


def fits(mesh):
    return mesh.shape["tm"] == 1 and mesh.shape["series"] == PLANES * IN_PLANE


def matmul(a, b):
    return jnp.dot(a, b, preferred_element_type=F32)


def matmul_t(a, b):
    return lax.dot_general(a, b, (((1,), (1,)), ((), ())), preferred_element_type=F32)


def kernel(
    taps_ref, x_hbm, cot_hbm, w_hbm, gi_hbm, grad_hbm,
    x, cot, w, gi, grad_ref,
    wide, xs, xt, pre, dk, g, s1, r1, s2a, s2b, r2a, r2b, s3a, s3b, r3a, r3b, s4, r4,
    load_sem, store_sem, ag_send, ag_recv, rs_send, rs_recv,
):
    series_n, time_n, width = x.shape
    flat = series_n * time_n
    span = 2 * DILATION_GAP
    rows = w.shape[0]
    group = IN_PLANE * rows
    half = width // 2
    tm = lax.axis_index("tm")
    me = lax.axis_index("series")
    core = lax.rem(me, 2)
    px = lax.rem(me // 2, 2)
    py = lax.rem(me // 4, 2)
    z = me // IN_PLANE

    def index(zz, yy, xx, cc):
        return ((zz * 2 + yy) * 2 + xx) * 2 + cc

    def block(zz, yy, xx, cc):
        return pl.ds(pl.multiple_of(index(zz, yy, xx, cc) * rows, 16), rows)

    to_x = (tm, index(z, py, 1 - px, core))
    to_y = (tm, index(z, 1 - py, px, core))
    to_c = (tm, index(z, py, px, 1 - core))
    to_z = [None] + [(tm, index(lax.rem(z + d, PLANES), py, px, core)) for d in (1, 2, 3)]

    loads = [
        pltpu.make_async_copy(src, dst, load_sem.at[i])
        for i, (src, dst) in enumerate([(w_hbm, w), (x_hbm, x), (cot_hbm, cot)])
    ]
    for c in loads:
        c.start()

    barrier = pltpu.get_barrier_semaphore()
    for dev in (to_x, to_y, to_c, *to_z[1:]):
        pl.semaphore_signal(barrier, inc=1, device_id=dev, device_id_type=MESH)

    loads[0].wait()
    own = block(z, py, px, core)
    wide[own, :] = w[...].astype(BF16)

    pl.semaphore_wait(barrier, 6)

    def start(src, dst, sems, k, dev):
        c = pltpu.make_async_remote_copy(
            src_ref=src, dst_ref=dst, send_sem=sems[0].at[k], recv_sem=sems[1].at[k],
            device_id=dev, device_id_type=MESH,
        )
        c.start()
        return c

    ag = (ag_send, ag_recv)
    rs = (rs_send, rs_recv)
    A, B, ALL = pl.ds(0, half), pl.ds(half, half), pl.ds(0, width)

    def pass_on(blk, cols, k, dev):
        return start(wide.at[blk, cols], wide.at[blk, cols], ag, k, dev)

    def before(j):
        return lax.rem(z + PLANES - j, PLANES)

    z_in = [None] + [pass_on(own, ALL, d, to_z[d]) for d in (1, 2, 3)]
    x1, y1, x2, y2, c_in = [], [], [], [], [[], [], [], []]

    def first_hop(j):
        if j:
            z_in[j].wait_recv()
        blk = block(before(j), py, px, core)
        x1.append(pass_on(blk, ALL, 4 + j, to_x))
        y1.append(pass_on(blk, ALL, 8 + j, to_y))
        c_in[j].append(pass_on(blk, ALL, 12 + j, to_c))

    def second_hop(j):
        x1[j].wait_recv()
        blk = block(before(j), py, 1 - px, core)
        y2.append(pass_on(blk, A, 16 + j, to_y))
        c_in[j].append(pass_on(blk, ALL, 20 + j, to_c))
        y1[j].wait_recv()
        blk = block(before(j), 1 - py, px, core)
        x2.append(pass_on(blk, B, 24 + j, to_x))
        c_in[j].append(pass_on(blk, ALL, 28 + j, to_c))

    def last_hop(j):
        y2[j].wait_recv()
        x2[j].wait_recv()
        c_in[j].append(pass_on(block(before(j), 1 - py, 1 - px, core), ALL, 32 + j, to_c))

    def forward(j):
        for c in c_in[j]:
            c.wait_recv()
        at = pl.ds(pl.multiple_of(before(j) * group, 128), group)
        term = matmul(xs[:, at], wide[at, :])
        pre[...] = term if j == 0 else pre[...] + term

    first_hop(0)
    tap = taps_ref[1]
    row = lax.broadcasted_iota(jnp.int32, (time_n, time_n), 0)
    column = lax.broadcasted_iota(jnp.int32, (time_n, time_n), 1)
    back = jnp.where(column == row - tap, 1.0, 0.0).astype(BF16)
    ahead = jnp.where(column == row + tap, 1.0, 0.0).astype(BF16)
    taps_at = [pl.ds(k * width, width) for k in range(3)]

    def shift(s):
        first = s * time_n
        at = pl.ds(first, time_n)
        xs[at, taps_at[0]] = x[s]
        xs[at, taps_at[1]] = matmul(back, x[s]).astype(BF16)
        xs[pl.ds(first, span), taps_at[2]] = jnp.zeros((span, width), BF16)
        xs[pl.ds(first + span, time_n - span), taps_at[2]] = x[s, pl.ds(0, time_n - span), :]

    def transpose(s, h):
        first = s * time_n
        at = pl.ds(first, time_n)
        turned = x[s, :, pl.ds(h * half, half)].T
        xt[pl.ds(h * half, half), at] = turned
        xt[pl.ds(width + h * half, half), at] = matmul(turned, ahead).astype(BF16)
        last = pl.ds(2 * width + h * half, half)
        xt[last, pl.ds(first, span)] = jnp.zeros((half, span), BF16)
        xt[last, pl.ds(first + span, time_n - span)] = turned[:, : time_n - span]

    loads[1].wait()
    shift(0)
    first_hop(1)
    second_hop(0)
    shift(1)
    first_hop(2)
    second_hop(1)
    last_hop(0)
    transpose(0, 0)
    first_hop(3)
    second_hop(2)
    last_hop(1)
    transpose(0, 1)
    second_hop(3)
    last_hop(2)
    forward(0)
    last_hop(3)
    transpose(1, 0)
    transpose(1, 1)
    forward(1)
    forward(2)
    loads[2].wait()
    for c in c_in[3]:
        c.wait_recv()
    at = pl.ds(pl.multiple_of(before(3) * group, 128), group)
    step = 256
    fine = 32
    for first in range(0, flat, step):
        part = pl.ds(first, step)
        total = pre[part, :] + matmul(xs[part, at], wide[at, :])
        for f in range(0, step, fine):
            t = total[f : f + fine]
            sig = 0.5 * jnp.tanh(0.5 * t) + 0.5
            up = cot[first // time_n, pl.ds(first % time_n + f, fine), :].astype(F32)
            dk[0, pl.ds(first + f, fine), :] = (up * (sig * (1.0 + t * (1.0 - sig)))).astype(BF16)

    c1, a2, b2, a3, b3, z4 = {}, {}, {}, {}, {}, {}

    def after(d):
        return lax.rem(z + d, PLANES)

    def weight_grad(d):
        zz = after(d)
        at = pl.ds(pl.multiple_of(zz * group, 128), group)
        g[at, :] = matmul(xt[at, :], dk[0])
        for q in range(4):
            s1[d, q] = g[block(zz, q // 2, q % 2, 1 - core), :].astype(BF16)
        c1[d] = start(s1.at[d], r1.at[d], rs, d, to_c)

    def both(d, yy, xx, cols):
        return g[block(after(d), yy, xx, core), cols] + r1[d, yy * 2 + xx, :, cols].astype(F32)

    def reduce_one(d):
        c1[d].wait_recv()
        for q in range(2):
            s2a[d, q] = both(d, q, 1 - px, A).astype(BF16)
            s2b[d, q] = both(d, 1 - py, q, B).astype(BF16)
        a2[d] = start(s2a.at[d], r2a.at[d], rs, 4 + d, to_x)
        b2[d] = start(s2b.at[d], r2b.at[d], rs, 8 + d, to_y)

    def reduce_two(d):
        a2[d].wait_recv()
        s3a[d] = (both(d, 1 - py, px, A) + r2a[d, 1 - py].astype(F32)).astype(BF16)
        a3[d] = start(s3a.at[d], r3a.at[d], rs, 12 + d, to_y)
        b2[d].wait_recv()
        s3b[d] = (both(d, py, 1 - px, B) + r2b[d, 1 - px].astype(F32)).astype(BF16)
        b3[d] = start(s3b.at[d], r3b.at[d], rs, 16 + d, to_x)

    def reduce_three(d):
        a3[d].wait_recv()
        b3[d].wait_recv()
        sum_a = both(d, py, px, A) + r2a[d, py].astype(F32) + r3a[d].astype(F32)
        sum_b = both(d, py, px, B) + r2b[d, px].astype(F32) + r3b[d].astype(F32)
        if d:
            s4[d - 1, :, A] = sum_a.astype(BF16)
            s4[d - 1, :, B] = sum_b.astype(BF16)
            z4[d] = start(s4.at[d - 1], r4.at[d - 1], rs, 19 + d, to_z[d])
        else:
            grad_ref[:, A] = sum_a
            grad_ref[:, B] = sum_b

    stores = []

    def shift_dpre(s):
        first = s * time_n
        dk[1, pl.ds(first, time_n), :] = matmul(ahead, dk[0, pl.ds(first, time_n), :]).astype(BF16)
        dk[2, pl.ds(first, time_n - span), :] = dk[0, pl.ds(first + span, time_n - span), :]
        dk[2, pl.ds(first + time_n - span, span), :] = jnp.zeros((span, width), BF16)

    def grad_input(i):
        size = time_n // 2
        s, first = i // 2, (i % 2) * size
        total = cot[s, pl.ds(first, size), :].astype(F32)
        for k in range(3):
            total = total + matmul_t(dk[k, pl.ds(i * size, size), :], wide[taps_at[k], :])
        gi[s, pl.ds(first, size), :] = total.astype(BF16)
        part = (s, pl.ds(first, size))
        c = pltpu.make_async_copy(gi.at[part], gi_hbm.at[part], store_sem.at[i])
        c.start()
        stores.append(c)

    o = (2, 1, 3, 0)
    weight_grad(o[0])
    weight_grad(o[1])
    reduce_one(o[0])
    weight_grad(o[2])
    reduce_one(o[1])
    weight_grad(o[3])
    reduce_one(o[2])
    shift_dpre(0)
    reduce_one(o[3])
    reduce_two(o[0])
    grad_input(0)
    reduce_two(o[1])
    reduce_three(o[0])
    grad_input(1)
    reduce_two(o[2])
    reduce_three(o[1])
    shift_dpre(1)
    reduce_two(o[3])
    reduce_three(o[2])
    grad_input(2)
    reduce_three(o[3])
    grad_input(3)
    total = grad_ref[...]
    for d in (2, 1, 3):
        z4[d].wait_recv()
        total = total + r4[d - 1].astype(F32)
    grad_ref[...] = total
    c = pltpu.make_async_copy(grad_ref, grad_hbm, store_sem.at[2 * series_n])
    c.start()
    stores.append(c)
    for c in z_in[1:] + x1 + y1 + x2 + y2 + sum(c_in, []):
        c.wait_send()
    for made in (c1, a2, b2, a3, b3, z4):
        for c in made.values():
            c.wait_send()
    for c in stores:
        c.wait()


def finish(
    gi, grad, weight, moment_one, second_moment_state, gi_out, nw_out, n1_out, n2_out,
    held, state, new, in_sem, out_sem, state_sem, new_sem,
):
    parts = [(s, pl.ds(h * held.shape[1] // 2, held.shape[1] // 2)) for s in range(held.shape[0]) for h in range(2)]
    inward = [pltpu.make_async_copy(gi.at[p], held.at[p], in_sem.at[i]) for i, p in enumerate(parts)]
    states = [
        pltpu.make_async_copy(src, state.at[i], state_sem.at[i])
        for i, src in enumerate((weight, grad, moment_one, second_moment_state))
    ]
    for c in inward + states:
        c.start()
    outward = []
    for i, p in enumerate(parts):
        inward[i].wait()
        outward.append(pltpu.make_async_copy(held.at[p], gi_out.at[p], out_sem.at[i]))
        outward[-1].start()
    for c in states:
        c.wait()
    new[0], new[1], new[2] = adamw(state[0], state[1], state[2], state[3])
    for i, dst in enumerate((nw_out, n1_out, n2_out)):
        outward.append(pltpu.make_async_copy(new.at[i], dst, new_sem.at[i]))
        outward[-1].start()
    for c in outward:
        c.wait()


def fused(inputs, cotangent, taps, weight, moment_one, second_moment_state):
    series_n, time_n, width = inputs.shape
    rows = weight.shape[0]
    depth = taps.shape[0] * width
    half = width // 2
    flat = series_n * time_n
    state = jax.ShapeDtypeStruct(weight.shape, F32)
    hbm = pl.BlockSpec(memory_space=pltpu.HBM)
    V = pltpu.VMEM
    gi, grad = pl.pallas_call(
        kernel,
        out_shape=[jax.ShapeDtypeStruct(inputs.shape, BF16), state],
        in_specs=[pl.BlockSpec(memory_space=pltpu.SMEM)] + [hbm] * 3,
        out_specs=[hbm] * 2,
        scratch_shapes=[
            V(inputs.shape, BF16), V(inputs.shape, BF16), V(weight.shape, F32),
            V(inputs.shape, BF16), V(weight.shape, F32),
            V((depth, width), BF16),
            V((flat, depth), BF16),
            V((depth, flat), BF16),
            V((flat, width), F32),
            V((3, flat, width), BF16),
            V((depth, width), F32),
            V((PLANES, 4, rows, width), BF16), V((PLANES, 4, rows, width), BF16),
            V((PLANES, 2, rows, half), BF16), V((PLANES, 2, rows, half), BF16),
            V((PLANES, 2, rows, half), BF16), V((PLANES, 2, rows, half), BF16),
            V((PLANES, rows, half), BF16), V((PLANES, rows, half), BF16),
            V((PLANES, rows, half), BF16), V((PLANES, rows, half), BF16),
            V((3, rows, width), BF16), V((3, rows, width), BF16),
            pltpu.SemaphoreType.DMA((3,)), pltpu.SemaphoreType.DMA((2 * series_n + 1,)),
            pltpu.SemaphoreType.DMA((36,)), pltpu.SemaphoreType.DMA((36,)),
            pltpu.SemaphoreType.DMA((23,)), pltpu.SemaphoreType.DMA((23,)),
        ],
        compiler_params=pltpu.CompilerParams(
            collective_id=0, has_side_effects=True, vmem_limit_bytes=63 * 1024 * 1024
        ),
        cost_estimate=pl.CostEstimate(
            flops=6 * flat * depth * width, bytes_accessed=6 * flat * width, transcendentals=flat * width
        ),
    )(taps, inputs, cotangent, weight)
    return tuple(pl.pallas_call(
        finish,
        out_shape=[jax.ShapeDtypeStruct(inputs.shape, BF16), state, state, state],
        in_specs=[hbm] * 5,
        out_specs=[hbm] * 4,
        scratch_shapes=[
            V(inputs.shape, BF16), V((4, rows, width), F32), V((3, rows, width), F32),
            pltpu.SemaphoreType.DMA((2 * series_n,)), pltpu.SemaphoreType.DMA((2 * series_n,)),
            pltpu.SemaphoreType.DMA((4,)), pltpu.SemaphoreType.DMA((3,)),
        ],
        compiler_params=pltpu.CompilerParams(vmem_limit_bytes=63 * 1024 * 1024),
        cost_estimate=pl.CostEstimate(flops=20 * rows * width, bytes_accessed=28 * rows * width, transcendentals=0),
    )(gi, grad, weight, moment_one, second_moment_state))


def solution(mesh):
    in_specs = (
        P("series", "tm", None),
        P("series", "tm", None),
        P(),
        P("series", None),
        P("series", None),
        P("series", None),
    )
    out_specs = (P("series", "tm", None), P("series", None), P("series", None), P("series", None))
    step = fused if fits(mesh) else body
    return jax.shard_map(step, mesh=mesh, in_specs=in_specs, out_specs=out_specs, check_vma=False)
```

```python
import functools

import jax
import jax.numpy as jnp
from jax import lax
from jax.experimental import pallas as pl
from jax.experimental.pallas import tpu as pltpu
from jax.sharding import PartitionSpec as P

DILATION_GAP = 64


def passed_along(array, axis, by):
    size = lax.axis_size(axis)
    pairs = [(i, i + by) for i in range(size) if 0 <= i + by < size]
    return lax.ppermute(array, axis, pairs)


def adamw(weight, grad, moment_one, second_moment_state):
    first = 0.9 * moment_one + 0.1 * grad
    second = 0.999 * second_moment_state + 0.001 * grad * grad
    unbiased_one = first / (1.0 - 0.9**10)
    unbiased_two = second / (1.0 - 0.999**10)
    updated = weight - 0.01 * (unbiased_one / (jnp.sqrt(unbiased_two) + 1e-08) + 0.1 * weight)
    return (updated, first, second)


def body(inputs, cotangent, taps, weight, moment_one, second_moment_state):
    series_n, time_n, width = inputs.shape
    tap_count = taps.shape[0]
    receptive_span = (tap_count - 1) * DILATION_GAP
    rows = series_n * time_n
    wide = lax.all_gather(weight.astype(jnp.bfloat16), "series", axis=0, tiled=True)
    earlier = passed_along(inputs[:, time_n - receptive_span :, :], "tm", 1)
    extended = jnp.concatenate([earlier, inputs], 1)
    shifted = [
        lax.dynamic_slice_in_dim(extended, receptive_span - taps[k], time_n, 1)
        for k in range(tap_count)
    ]
    stacked = jnp.concatenate(shifted, 2).reshape(rows, tap_count * width)
    pre = jnp.dot(stacked, wide, preferred_element_type=jnp.float32)
    sig = jax.nn.sigmoid(pre)
    upstream = cotangent.reshape(rows, width)
    dpre_flat = (upstream.astype(jnp.float32) * (sig * (1.0 + pre * (1.0 - sig)))).astype(
        jnp.bfloat16
    )
    dpre = dpre_flat.reshape(series_n, time_n, width)
    ahead = passed_along(dpre[:, :receptive_span, :], "tm", -1)
    later = jnp.concatenate([dpre, ahead], 1)
    result = upstream.astype(jnp.float32)
    for k in range(tap_count):
        moved = lax.dynamic_slice_in_dim(later, taps[k], time_n, 1).reshape(rows, width)
        result = result + lax.dot_general(
            moved,
            wide[k * width : (k + 1) * width],
            (((1,), (1,)), ((), ())),
            preferred_element_type=jnp.float32,
        )
    grad_input = result.astype(jnp.bfloat16).reshape(series_n, time_n, width)
    grad_shard = lax.psum_scatter(
        lax.dot_general(
            stacked, dpre_flat, (((0,), (0,)), ((), ())), preferred_element_type=jnp.float32
        ),
        "series",
        scatter_dimension=0,
        tiled=True,
    )
    grad_shard = lax.psum(grad_shard, "tm")
    new_weight, new_moment_one, new_moment_two = adamw(
        weight, grad_shard, moment_one, second_moment_state
    )
    return (grad_input, new_weight, new_moment_one, new_moment_two)


MESH = pl.DeviceIdType.MESH
F32, BF16 = jnp.float32, jnp.bfloat16
PLANES, IN_PLANE = 4, 8


def fits(mesh):
    return mesh.shape["tm"] == 1 and mesh.shape["series"] == PLANES * IN_PLANE


def matmul(a, b):
    return jnp.dot(a, b, preferred_element_type=F32)


def matmul_t(a, b):
    return lax.dot_general(a, b, (((1,), (1,)), ((), ())), preferred_element_type=F32)


def kernel(
    taps_ref, x_hbm, cot_hbm, w_hbm, gi_hbm, grad_hbm,
    x, cot, w, gi, grad_ref,
    wide, xs, xt, pre, dk, g, s1, r1, s2, r2, s3, r3,
    load_sem, store_sem, ag_send, ag_recv, rs_send, rs_recv,
):
    series_n, time_n, width = x.shape
    flat = series_n * time_n
    span = 2 * DILATION_GAP
    rows = w.shape[0]
    group = IN_PLANE * rows
    half = width // 2
    tm = lax.axis_index("tm")
    me = lax.axis_index("series")
    core = lax.rem(me, 2)
    px = lax.rem(me // 2, 2)
    py = lax.rem(me // 4, 2)
    z = me // IN_PLANE

    def index(zz, yy, xx, cc):
        return ((zz * 2 + yy) * 2 + xx) * 2 + cc

    def block(zz, yy, xx, cc):
        return pl.ds(pl.multiple_of(index(zz, yy, xx, cc) * rows, 16), rows)

    to_x = (tm, index(z, py, 1 - px, core))
    to_y = (tm, index(z, 1 - py, px, core))
    to_d = (tm, index(z, 1 - py, 1 - px, core))
    to_c = (tm, index(z, py, px, 1 - core))
    to_z = [None] + [(tm, index(lax.rem(z + d, PLANES), py, px, core)) for d in (1, 2, 3)]

    loads = [
        pltpu.make_async_copy(src, dst, load_sem.at[i])
        for i, (src, dst) in enumerate([(w_hbm, w), (x_hbm, x), (cot_hbm, cot)])
    ]
    loads[0].start()

    barrier = pltpu.get_barrier_semaphore()
    for dev in (to_x, to_y, to_d, to_c, *to_z[1:]):
        pl.semaphore_signal(barrier, inc=1, device_id=dev, device_id_type=MESH)

    loads[0].wait()
    own = block(z, py, px, core)
    wide[own, :] = w[...].astype(BF16)

    pl.semaphore_wait(barrier, 7)

    def start(src, dst, sems, k, dev):
        c = pltpu.make_async_remote_copy(
            src_ref=src, dst_ref=dst, send_sem=sems[0].at[k], recv_sem=sems[1].at[k],
            device_id=dev, device_id_type=MESH,
        )
        c.start()
        return c

    ag = (ag_send, ag_recv)
    rs = (rs_send, rs_recv)

    def pass_on(blk, k, dev):
        return start(wide.at[blk, :], wide.at[blk, :], ag, k, dev)

    def before(j):
        return lax.rem(z + PLANES - j, PLANES)

    z_in = [None] + [pass_on(own, d, to_z[d]) for d in (1, 2, 3)]
    plane = [(to_x, py, 1 - px), (to_y, 1 - py, px), (to_d, 1 - py, 1 - px)]
    p_in, c_in = [], [[], [], [], []]

    def first_hop(j):
        if j:
            z_in[j].wait_recv()
        blk = block(before(j), py, px, core)
        p_in.append([pass_on(blk, 4 + 4 * i + j, to) for i, (to, _, _) in enumerate(plane)])
        c_in[j].append(pass_on(blk, 16 + j, to_c))

    def second_hop(j):
        for i, (_, yy, xx) in enumerate(plane):
            p_in[j][i].wait_recv()
            c_in[j].append(pass_on(block(before(j), yy, xx, core), 20 + 4 * i + j, to_c))

    def forward(j):
        for c in c_in[j]:
            c.wait_recv()
        at = pl.ds(pl.multiple_of(before(j) * group, 128), group)
        term = matmul(xs[:, at], wide[at, :])
        pre[...] = term if j == 0 else pre[...] + term

    first_hop(0)
    loads[1].start()
    tap = taps_ref[1]
    row = lax.broadcasted_iota(jnp.int32, (time_n, time_n), 0)
    column = lax.broadcasted_iota(jnp.int32, (time_n, time_n), 1)
    back = jnp.where(column == row - tap, 1.0, 0.0).astype(BF16)
    ahead = jnp.where(column == row + tap, 1.0, 0.0).astype(BF16)
    taps_at = [pl.ds(k * width, width) for k in range(3)]

    def shift(s):
        first = s * time_n
        at = pl.ds(first, time_n)
        xs[at, taps_at[0]] = x[s]
        xs[at, taps_at[1]] = matmul(back, x[s]).astype(BF16)
        xs[pl.ds(first, span), taps_at[2]] = jnp.zeros((span, width), BF16)
        xs[pl.ds(first + span, time_n - span), taps_at[2]] = x[s, pl.ds(0, time_n - span), :]

    def transpose(s, h):
        first = s * time_n
        at = pl.ds(first, time_n)
        turned = x[s, :, pl.ds(h * half, half)].T
        xt[pl.ds(h * half, half), at] = turned
        xt[pl.ds(width + h * half, half), at] = matmul(turned, ahead).astype(BF16)
        last = pl.ds(2 * width + h * half, half)
        xt[last, pl.ds(first, span)] = jnp.zeros((half, span), BF16)
        xt[last, pl.ds(first + span, time_n - span)] = turned[:, : time_n - span]

    first_hop(1)
    loads[1].wait()
    loads[2].start()
    shift(0)
    first_hop(2)
    second_hop(0)
    shift(1)
    first_hop(3)
    second_hop(1)
    transpose(0, 0)
    second_hop(2)
    forward(0)
    transpose(0, 1)
    second_hop(3)
    transpose(1, 0)
    transpose(1, 1)
    forward(1)
    forward(2)
    loads[2].wait()
    for c in c_in[3]:
        c.wait_recv()
    at = pl.ds(pl.multiple_of(before(3) * group, 128), group)
    step = 256
    fine = 32
    for first in range(0, flat, step):
        part = pl.ds(first, step)
        total = pre[part, :] + matmul(xs[part, at], wide[at, :])
        for f in range(0, step, fine):
            t = total[f : f + fine]
            sig = 0.5 * jnp.tanh(0.5 * t) + 0.5
            up = cot[first // time_n, pl.ds(first % time_n + f, fine), :].astype(F32)
            dk[0, pl.ds(first + f, fine), :] = (up * (sig * (1.0 + t * (1.0 - sig)))).astype(BF16)

    c1, p2, z4 = {}, {}, {}

    def after(d):
        return lax.rem(z + d, PLANES)

    def weight_grad(d):
        zz = after(d)
        at = pl.ds(pl.multiple_of(zz * group, 128), group)
        g[at, :] = matmul(xt[at, :], dk[0])
        for q in range(4):
            s1[d, q] = g[block(zz, q // 2, q % 2, 1 - core), :].astype(BF16)
        c1[d] = start(s1.at[d], r1.at[d], rs, d, to_c)

    def chip_sum(d, yy, xx):
        return g[block(after(d), yy, xx, core), :] + r1[d, yy * 2 + xx].astype(F32)

    def reduce_one(d):
        c1[d].wait_recv()
        p2[d] = []
        for i, (to, yy, xx) in enumerate(plane):
            s2[d, i] = chip_sum(d, yy, xx).astype(BF16)
            p2[d].append(start(s2.at[d, i], r2.at[d, i], rs, 4 + 3 * d + i, to))

    def reduce_two(d):
        total = chip_sum(d, py, px)
        for i in range(3):
            p2[d][i].wait_recv()
            total = total + r2[d, i].astype(F32)
        if d:
            s3[d - 1] = total.astype(BF16)
            z4[d] = start(s3.at[d - 1], r3.at[d - 1], rs, 15 + d, to_z[d])
        else:
            grad_ref[...] = total

    stores = []

    def shift_dpre(s):
        first = s * time_n
        dk[1, pl.ds(first, time_n), :] = matmul(ahead, dk[0, pl.ds(first, time_n), :]).astype(BF16)
        dk[2, pl.ds(first, time_n - span), :] = dk[0, pl.ds(first + span, time_n - span), :]
        dk[2, pl.ds(first + time_n - span, span), :] = jnp.zeros((span, width), BF16)

    def grad_input(i):
        size = time_n // 2
        s, first = i // 2, (i % 2) * size
        total = cot[s, pl.ds(first, size), :].astype(F32)
        for k in range(3):
            total = total + matmul_t(dk[k, pl.ds(i * size, size), :], wide[taps_at[k], :])
        gi[s, pl.ds(first, size), :] = total.astype(BF16)
        part = (s, pl.ds(first, size))
        c = pltpu.make_async_copy(gi.at[part], gi_hbm.at[part], store_sem.at[i])
        c.start()
        stores.append(c)

    o = (2, 1, 3, 0)
    weight_grad(o[0])
    weight_grad(o[1])
    reduce_one(o[0])
    weight_grad(o[2])
    reduce_one(o[1])
    weight_grad(o[3])
    reduce_one(o[2])
    reduce_one(o[3])
    shift_dpre(0)
    reduce_two(o[0])
    grad_input(0)
    reduce_two(o[1])
    grad_input(1)
    reduce_two(o[2])
    shift_dpre(1)
    reduce_two(o[3])
    grad_input(2)
    grad_input(3)
    total = grad_ref[...]
    for d in (2, 1, 3):
        z4[d].wait_recv()
        total = total + r3[d - 1].astype(F32)
    grad_ref[...] = total
    c = pltpu.make_async_copy(grad_ref, grad_hbm, store_sem.at[2 * series_n])
    c.start()
    stores.append(c)
    for c in z_in[1:] + sum(p_in, []) + sum(c_in, []) + sum(p2.values(), []):
        c.wait_send()
    for made in (c1, z4):
        for c in made.values():
            c.wait_send()
    for c in stores:
        c.wait()


def finish(
    gi, grad, weight, moment_one, second_moment_state, gi_out, nw_out, n1_out, n2_out,
    held, state, new, in_sem, out_sem, state_sem, new_sem,
):
    parts = [(s, pl.ds(h * held.shape[1] // 2, held.shape[1] // 2)) for s in range(held.shape[0]) for h in range(2)]
    inward = [pltpu.make_async_copy(gi.at[p], held.at[p], in_sem.at[i]) for i, p in enumerate(parts)]
    states = [
        pltpu.make_async_copy(src, state.at[i], state_sem.at[i])
        for i, src in enumerate((weight, grad, moment_one, second_moment_state))
    ]
    for c in inward + states:
        c.start()
    outward = []
    for i, p in enumerate(parts):
        inward[i].wait()
        outward.append(pltpu.make_async_copy(held.at[p], gi_out.at[p], out_sem.at[i]))
        outward[-1].start()
    for c in states:
        c.wait()
    new[0], new[1], new[2] = adamw(state[0], state[1], state[2], state[3])
    for i, dst in enumerate((nw_out, n1_out, n2_out)):
        outward.append(pltpu.make_async_copy(new.at[i], dst, new_sem.at[i]))
        outward[-1].start()
    for c in outward:
        c.wait()


def fused(inputs, cotangent, taps, weight, moment_one, second_moment_state):
    series_n, time_n, width = inputs.shape
    rows = weight.shape[0]
    depth = taps.shape[0] * width
    flat = series_n * time_n
    state = jax.ShapeDtypeStruct(weight.shape, F32)
    hbm = pl.BlockSpec(memory_space=pltpu.HBM)
    V = pltpu.VMEM
    gi, grad = pl.pallas_call(
        kernel,
        out_shape=[jax.ShapeDtypeStruct(inputs.shape, BF16), state],
        in_specs=[pl.BlockSpec(memory_space=pltpu.SMEM)] + [hbm] * 3,
        out_specs=[hbm] * 2,
        scratch_shapes=[
            V(inputs.shape, BF16), V(inputs.shape, BF16), V(weight.shape, F32),
            V(inputs.shape, BF16), V(weight.shape, F32),
            V((depth, width), BF16),
            V((flat, depth), BF16),
            V((depth, flat), BF16),
            V((flat, width), F32),
            V((3, flat, width), BF16),
            V((depth, width), F32),
            V((PLANES, 4, rows, width), BF16), V((PLANES, 4, rows, width), BF16),
            V((PLANES, 3, rows, width), BF16), V((PLANES, 3, rows, width), BF16),
            V((3, rows, width), BF16), V((3, rows, width), BF16),
            pltpu.SemaphoreType.DMA((3,)), pltpu.SemaphoreType.DMA((2 * series_n + 1,)),
            pltpu.SemaphoreType.DMA((32,)), pltpu.SemaphoreType.DMA((32,)),
            pltpu.SemaphoreType.DMA((19,)), pltpu.SemaphoreType.DMA((19,)),
        ],
        compiler_params=pltpu.CompilerParams(
            collective_id=0, has_side_effects=True, vmem_limit_bytes=63 * 1024 * 1024
        ),
        cost_estimate=pl.CostEstimate(
            flops=6 * flat * depth * width, bytes_accessed=6 * flat * width, transcendentals=flat * width
        ),
    )(taps, inputs, cotangent, weight)
    return tuple(pl.pallas_call(
        finish,
        out_shape=[jax.ShapeDtypeStruct(inputs.shape, BF16), state, state, state],
        in_specs=[hbm] * 5,
        out_specs=[hbm] * 4,
        scratch_shapes=[
            V(inputs.shape, BF16), V((4, rows, width), F32), V((3, rows, width), F32),
            pltpu.SemaphoreType.DMA((2 * series_n,)), pltpu.SemaphoreType.DMA((2 * series_n,)),
            pltpu.SemaphoreType.DMA((4,)), pltpu.SemaphoreType.DMA((3,)),
        ],
        compiler_params=pltpu.CompilerParams(vmem_limit_bytes=63 * 1024 * 1024),
        cost_estimate=pl.CostEstimate(flops=20 * rows * width, bytes_accessed=28 * rows * width, transcendentals=0),
    )(gi, grad, weight, moment_one, second_moment_state))


def solution(mesh):
    in_specs = (
        P("series", "tm", None),
        P("series", "tm", None),
        P(),
        P("series", None),
        P("series", None),
        P("series", None),
    )
    out_specs = (P("series", "tm", None), P("series", None), P("series", None), P("series", None))
    step = fused if fits(mesh) else body
    return jax.shard_map(step, mesh=mesh, in_specs=in_specs, out_specs=out_specs, check_vma=False)
```

```python
import functools

import jax
import jax.numpy as jnp
from jax import lax
from jax.experimental import pallas as pl
from jax.experimental.pallas import tpu as pltpu
from jax.sharding import PartitionSpec as P

DILATION_GAP = 64


def passed_along(array, axis, by):
    size = lax.axis_size(axis)
    pairs = [(i, i + by) for i in range(size) if 0 <= i + by < size]
    return lax.ppermute(array, axis, pairs)


def adamw(weight, grad, moment_one, second_moment_state):
    first = 0.9 * moment_one + 0.1 * grad
    second = 0.999 * second_moment_state + 0.001 * grad * grad
    unbiased_one = first / (1.0 - 0.9**10)
    unbiased_two = second / (1.0 - 0.999**10)
    updated = weight - 0.01 * (unbiased_one / (jnp.sqrt(unbiased_two) + 1e-08) + 0.1 * weight)
    return (updated, first, second)


def body(inputs, cotangent, taps, weight, moment_one, second_moment_state):
    series_n, time_n, width = inputs.shape
    tap_count = taps.shape[0]
    receptive_span = (tap_count - 1) * DILATION_GAP
    rows = series_n * time_n
    wide = lax.all_gather(weight.astype(jnp.bfloat16), "series", axis=0, tiled=True)
    earlier = passed_along(inputs[:, time_n - receptive_span :, :], "tm", 1)
    extended = jnp.concatenate([earlier, inputs], 1)
    shifted = [
        lax.dynamic_slice_in_dim(extended, receptive_span - taps[k], time_n, 1)
        for k in range(tap_count)
    ]
    stacked = jnp.concatenate(shifted, 2).reshape(rows, tap_count * width)
    pre = jnp.dot(stacked, wide, preferred_element_type=jnp.float32)
    sig = jax.nn.sigmoid(pre)
    upstream = cotangent.reshape(rows, width)
    dpre_flat = (upstream.astype(jnp.float32) * (sig * (1.0 + pre * (1.0 - sig)))).astype(
        jnp.bfloat16
    )
    dpre = dpre_flat.reshape(series_n, time_n, width)
    ahead = passed_along(dpre[:, :receptive_span, :], "tm", -1)
    later = jnp.concatenate([dpre, ahead], 1)
    result = upstream.astype(jnp.float32)
    for k in range(tap_count):
        moved = lax.dynamic_slice_in_dim(later, taps[k], time_n, 1).reshape(rows, width)
        result = result + lax.dot_general(
            moved,
            wide[k * width : (k + 1) * width],
            (((1,), (1,)), ((), ())),
            preferred_element_type=jnp.float32,
        )
    grad_input = result.astype(jnp.bfloat16).reshape(series_n, time_n, width)
    grad_shard = lax.psum_scatter(
        lax.dot_general(
            stacked, dpre_flat, (((0,), (0,)), ((), ())), preferred_element_type=jnp.float32
        ),
        "series",
        scatter_dimension=0,
        tiled=True,
    )
    grad_shard = lax.psum(grad_shard, "tm")
    new_weight, new_moment_one, new_moment_two = adamw(
        weight, grad_shard, moment_one, second_moment_state
    )
    return (grad_input, new_weight, new_moment_one, new_moment_two)


MESH = pl.DeviceIdType.MESH
F32, BF16 = jnp.float32, jnp.bfloat16
PLANES, IN_PLANE = 4, 8


def fits(mesh):
    return mesh.shape["tm"] == 1 and mesh.shape["series"] == PLANES * IN_PLANE


def matmul(a, b):
    return jnp.dot(a, b, preferred_element_type=F32)


def matmul_t(a, b):
    return lax.dot_general(a, b, (((1,), (1,)), ((), ())), preferred_element_type=F32)


def kernel(
    taps_ref, x_hbm, cot_hbm, w_hbm, gi_hbm, grad_hbm,
    x, cot, w, gi, grad_ref,
    wide, xs, xt, pre, dk, g, s1, r1, s2, r2, s3, r3,
    load_sem, store_sem, ag_send, ag_recv, rs_send, rs_recv,
):
    series_n, time_n, width = x.shape
    flat = series_n * time_n
    span = 2 * DILATION_GAP
    rows = w.shape[0]
    group = IN_PLANE * rows
    half = width // 2
    tm = lax.axis_index("tm")
    me = lax.axis_index("series")
    core = lax.rem(me, 2)
    px = lax.rem(me // 2, 2)
    py = lax.rem(me // 4, 2)
    z = me // IN_PLANE

    def index(zz, yy, xx, cc):
        return ((zz * 2 + yy) * 2 + xx) * 2 + cc

    def block(zz, yy, xx, cc):
        return pl.ds(pl.multiple_of(index(zz, yy, xx, cc) * rows, 16), rows)

    to_x = (tm, index(z, py, 1 - px, core))
    to_y = (tm, index(z, 1 - py, px, core))
    to_d = (tm, index(z, 1 - py, 1 - px, core))
    to_c = (tm, index(z, py, px, 1 - core))
    to_z = [None] + [(tm, index(lax.rem(z + d, PLANES), py, px, core)) for d in (1, 2, 3)]

    loads = [
        pltpu.make_async_copy(src, dst, load_sem.at[i])
        for i, (src, dst) in enumerate([(w_hbm, w), (x_hbm, x), (cot_hbm, cot)])
    ]
    loads[0].start()

    barrier = pltpu.get_barrier_semaphore()
    for dev in (to_x, to_y, to_d, to_c, *to_z[1:]):
        pl.semaphore_signal(barrier, inc=1, device_id=dev, device_id_type=MESH)

    loads[0].wait()
    own = block(z, py, px, core)
    wide[own, :] = w[...].astype(BF16)

    pl.semaphore_wait(barrier, 7)

    def start(src, dst, sems, k, dev):
        c = pltpu.make_async_remote_copy(
            src_ref=src, dst_ref=dst, send_sem=sems[0].at[k], recv_sem=sems[1].at[k],
            device_id=dev, device_id_type=MESH,
        )
        c.start()
        return c

    ag = (ag_send, ag_recv)
    rs = (rs_send, rs_recv)

    def pass_on(blk, k, dev):
        return start(wide.at[blk, :], wide.at[blk, :], ag, k, dev)

    def before(j):
        return lax.rem(z + PLANES - j, PLANES)

    z_in = [None] + [pass_on(own, d, to_z[d]) for d in (1, 2, 3)]
    plane = [(to_x, py, 1 - px), (to_y, 1 - py, px), (to_d, 1 - py, 1 - px)]
    p_in, c_in = [], [[], [], [], []]

    def first_hop(j):
        if j:
            z_in[j].wait_recv()
        blk = block(before(j), py, px, core)
        p_in.append([pass_on(blk, 4 + 4 * i + j, to) for i, (to, _, _) in enumerate(plane)])
        c_in[j].append(pass_on(blk, 16 + j, to_c))

    def second_hop(j):
        for i, (_, yy, xx) in enumerate(plane):
            p_in[j][i].wait_recv()
            c_in[j].append(pass_on(block(before(j), yy, xx, core), 20 + 4 * i + j, to_c))

    def forward(j):
        for c in c_in[j]:
            c.wait_recv()
        at = pl.ds(pl.multiple_of(before(j) * group, 128), group)
        term = matmul(xs[:, at], wide[at, :])
        pre[...] = term if j == 0 else pre[...] + term

    first_hop(0)
    loads[1].start()
    tap = taps_ref[1]
    row = lax.broadcasted_iota(jnp.int32, (time_n, time_n), 0)
    column = lax.broadcasted_iota(jnp.int32, (time_n, time_n), 1)
    back = jnp.where(column == row - tap, 1.0, 0.0).astype(BF16)
    ahead = jnp.where(column == row + tap, 1.0, 0.0).astype(BF16)
    taps_at = [pl.ds(k * width, width) for k in range(3)]

    def shift(s):
        first = s * time_n
        at = pl.ds(first, time_n)
        xs[at, taps_at[0]] = x[s]
        xs[at, taps_at[1]] = matmul(back, x[s]).astype(BF16)
        xs[pl.ds(first, span), taps_at[2]] = jnp.zeros((span, width), BF16)
        xs[pl.ds(first + span, time_n - span), taps_at[2]] = x[s, pl.ds(0, time_n - span), :]

    def transpose(s, h):
        first = s * time_n
        at = pl.ds(first, time_n)
        turned = x[s, :, pl.ds(h * half, half)].T
        xt[pl.ds(h * half, half), at] = turned
        xt[pl.ds(width + h * half, half), at] = matmul(turned, ahead).astype(BF16)
        last = pl.ds(2 * width + h * half, half)
        xt[last, pl.ds(first, span)] = jnp.zeros((half, span), BF16)
        xt[last, pl.ds(first + span, time_n - span)] = turned[:, : time_n - span]

    first_hop(1)
    loads[1].wait()
    loads[2].start()
    shift(0)
    first_hop(2)
    transpose(0, 0)
    first_hop(3)
    second_hop(0)
    shift(1)
    second_hop(1)
    transpose(0, 1)
    forward(0)
    second_hop(2)
    transpose(1, 0)
    forward(1)
    second_hop(3)
    transpose(1, 1)
    forward(2)
    loads[2].wait()
    for c in c_in[3]:
        c.wait_recv()
    at = pl.ds(pl.multiple_of(before(3) * group, 128), group)
    step = 256
    fine = 32
    for first in range(0, flat, step):
        part = pl.ds(first, step)
        total = pre[part, :] + matmul(xs[part, at], wide[at, :])
        for f in range(0, step, fine):
            t = total[f : f + fine]
            sig = 0.5 * jnp.tanh(0.5 * t) + 0.5
            up = cot[first // time_n, pl.ds(first % time_n + f, fine), :].astype(F32)
            dk[0, pl.ds(first + f, fine), :] = (up * (sig * (1.0 + t * (1.0 - sig)))).astype(BF16)

    c1, p2, z4 = {}, {}, {}

    def after(d):
        return lax.rem(z + d, PLANES)

    def weight_grad(d):
        zz = after(d)
        at = pl.ds(pl.multiple_of(zz * group, 128), group)
        g[at, :] = matmul(xt[at, :], dk[0])
        for q in range(4):
            s1[d, q] = g[block(zz, q // 2, q % 2, 1 - core), :].astype(BF16)
        c1[d] = start(s1.at[d], r1.at[d], rs, d, to_c)

    def chip_sum(d, yy, xx):
        return g[block(after(d), yy, xx, core), :] + r1[d, yy * 2 + xx].astype(F32)

    def reduce_one(d):
        c1[d].wait_recv()
        p2[d] = []
        for i, (to, yy, xx) in enumerate(plane):
            s2[d, i] = chip_sum(d, yy, xx).astype(BF16)
            p2[d].append(start(s2.at[d, i], r2.at[d, i], rs, 4 + 3 * d + i, to))

    def reduce_two(d):
        total = chip_sum(d, py, px)
        for i in range(3):
            p2[d][i].wait_recv()
            total = total + r2[d, i].astype(F32)
        if d:
            s3[d - 1] = total.astype(BF16)
            z4[d] = start(s3.at[d - 1], r3.at[d - 1], rs, 15 + d, to_z[d])
        else:
            grad_ref[...] = total

    stores = []

    def shift_dpre(s):
        first = s * time_n
        dk[1, pl.ds(first, time_n), :] = matmul(ahead, dk[0, pl.ds(first, time_n), :]).astype(BF16)

    def static_shift_dpre(s):
        first = s * time_n
        dk[2, pl.ds(first, time_n - span), :] = dk[0, pl.ds(first + span, time_n - span), :]
        dk[2, pl.ds(first + time_n - span, span), :] = jnp.zeros((span, width), BF16)

    def grad_input(k):
        term = matmul_t(dk[k], wide[taps_at[k], :])
        for s in range(series_n):
            part = pl.ds(s * time_n, time_n)
            mine = term[s * time_n : (s + 1) * time_n]
            if k == 0:
                pre[part, :] = cot[s].astype(F32) + mine
            elif k == 2:
                pre[part, :] = pre[part, :] + mine
            else:
                gi[s] = (pre[part, :] + mine).astype(BF16)
                c = pltpu.make_async_copy(gi.at[s], gi_hbm.at[s], store_sem.at[s])
                c.start()
                stores.append(c)

    o = (2, 1, 3, 0)
    weight_grad(o[0])
    weight_grad(o[1])
    reduce_one(o[0])
    weight_grad(o[2])
    reduce_one(o[1])
    weight_grad(o[3])
    reduce_one(o[2])
    reduce_one(o[3])
    grad_input(0)
    reduce_two(o[0])
    for s in range(series_n):
        static_shift_dpre(s)
    grad_input(2)
    reduce_two(o[1])
    for s in range(series_n):
        shift_dpre(s)
    reduce_two(o[2])
    reduce_two(o[3])
    grad_input(1)
    total = grad_ref[...]
    for d in (2, 1, 3):
        z4[d].wait_recv()
        total = total + r3[d - 1].astype(F32)
    grad_ref[...] = total
    c = pltpu.make_async_copy(grad_ref, grad_hbm, store_sem.at[series_n])
    c.start()
    stores.append(c)
    for c in z_in[1:] + sum(p_in, []) + sum(c_in, []) + sum(p2.values(), []):
        c.wait_send()
    for made in (c1, z4):
        for c in made.values():
            c.wait_send()
    for c in stores:
        c.wait()


def finish(
    gi, grad, weight, moment_one, second_moment_state, gi_out, nw_out, n1_out, n2_out,
    held, state, new, in_sem, out_sem, state_sem, new_sem,
):
    parts = [(s, pl.ds(h * held.shape[1] // 2, held.shape[1] // 2)) for s in range(held.shape[0]) for h in range(2)]
    inward = [pltpu.make_async_copy(gi.at[p], held.at[p], in_sem.at[i]) for i, p in enumerate(parts)]
    states = [
        pltpu.make_async_copy(src, state.at[i], state_sem.at[i])
        for i, src in enumerate((weight, grad, moment_one, second_moment_state))
    ]
    for c in inward + states:
        c.start()
    outward = []
    for i, p in enumerate(parts):
        inward[i].wait()
        outward.append(pltpu.make_async_copy(held.at[p], gi_out.at[p], out_sem.at[i]))
        outward[-1].start()
    for c in states:
        c.wait()
    new[0], new[1], new[2] = adamw(state[0], state[1], state[2], state[3])
    for i, dst in enumerate((nw_out, n1_out, n2_out)):
        outward.append(pltpu.make_async_copy(new.at[i], dst, new_sem.at[i]))
        outward[-1].start()
    for c in outward:
        c.wait()


def fused(inputs, cotangent, taps, weight, moment_one, second_moment_state):
    series_n, time_n, width = inputs.shape
    rows = weight.shape[0]
    depth = taps.shape[0] * width
    flat = series_n * time_n
    state = jax.ShapeDtypeStruct(weight.shape, F32)
    hbm = pl.BlockSpec(memory_space=pltpu.HBM)
    V = pltpu.VMEM
    gi, grad = pl.pallas_call(
        kernel,
        out_shape=[jax.ShapeDtypeStruct(inputs.shape, BF16), state],
        in_specs=[pl.BlockSpec(memory_space=pltpu.SMEM)] + [hbm] * 3,
        out_specs=[hbm] * 2,
        scratch_shapes=[
            V(inputs.shape, BF16), V(inputs.shape, BF16), V(weight.shape, F32),
            V(inputs.shape, BF16), V(weight.shape, F32),
            V((depth, width), BF16),
            V((flat, depth), BF16),
            V((depth, flat), BF16),
            V((flat, width), F32),
            V((3, flat, width), BF16),
            V((depth, width), F32),
            V((PLANES, 4, rows, width), BF16), V((PLANES, 4, rows, width), BF16),
            V((PLANES, 3, rows, width), BF16), V((PLANES, 3, rows, width), BF16),
            V((3, rows, width), BF16), V((3, rows, width), BF16),
            pltpu.SemaphoreType.DMA((3,)), pltpu.SemaphoreType.DMA((series_n + 1,)),
            pltpu.SemaphoreType.DMA((32,)), pltpu.SemaphoreType.DMA((32,)),
            pltpu.SemaphoreType.DMA((19,)), pltpu.SemaphoreType.DMA((19,)),
        ],
        compiler_params=pltpu.CompilerParams(
            collective_id=0, has_side_effects=True, vmem_limit_bytes=63 * 1024 * 1024
        ),
        cost_estimate=pl.CostEstimate(
            flops=6 * flat * depth * width, bytes_accessed=6 * flat * width, transcendentals=flat * width
        ),
    )(taps, inputs, cotangent, weight)
    return tuple(pl.pallas_call(
        finish,
        out_shape=[jax.ShapeDtypeStruct(inputs.shape, BF16), state, state, state],
        in_specs=[hbm] * 5,
        out_specs=[hbm] * 4,
        scratch_shapes=[
            V(inputs.shape, BF16), V((4, rows, width), F32), V((3, rows, width), F32),
            pltpu.SemaphoreType.DMA((2 * series_n,)), pltpu.SemaphoreType.DMA((2 * series_n,)),
            pltpu.SemaphoreType.DMA((4,)), pltpu.SemaphoreType.DMA((3,)),
        ],
        compiler_params=pltpu.CompilerParams(vmem_limit_bytes=63 * 1024 * 1024),
        cost_estimate=pl.CostEstimate(flops=20 * rows * width, bytes_accessed=28 * rows * width, transcendentals=0),
    )(gi, grad, weight, moment_one, second_moment_state))


def solution(mesh):
    in_specs = (
        P("series", "tm", None),
        P("series", "tm", None),
        P(),
        P("series", None),
        P("series", None),
        P("series", None),
    )
    out_specs = (P("series", "tm", None), P("series", None), P("series", None), P("series", None))
    step = fused if fits(mesh) else body
    return jax.shard_map(step, mesh=mesh, in_specs=in_specs, out_specs=out_specs, check_vma=False)
```

```python
import functools

import jax
import jax.numpy as jnp
from jax import lax
from jax.experimental import pallas as pl
from jax.experimental.pallas import tpu as pltpu
from jax.sharding import PartitionSpec as P

DILATION_GAP = 64


def passed_along(array, axis, by):
    size = lax.axis_size(axis)
    pairs = [(i, i + by) for i in range(size) if 0 <= i + by < size]
    return lax.ppermute(array, axis, pairs)


def adamw(weight, grad, moment_one, second_moment_state):
    first = 0.9 * moment_one + 0.1 * grad
    second = 0.999 * second_moment_state + 0.001 * grad * grad
    unbiased_one = first / (1.0 - 0.9**10)
    unbiased_two = second / (1.0 - 0.999**10)
    updated = weight - 0.01 * (unbiased_one / (jnp.sqrt(unbiased_two) + 1e-08) + 0.1 * weight)
    return (updated, first, second)


def body(inputs, cotangent, taps, weight, moment_one, second_moment_state):
    series_n, time_n, width = inputs.shape
    tap_count = taps.shape[0]
    receptive_span = (tap_count - 1) * DILATION_GAP
    rows = series_n * time_n
    wide = lax.all_gather(weight.astype(jnp.bfloat16), "series", axis=0, tiled=True)
    earlier = passed_along(inputs[:, time_n - receptive_span :, :], "tm", 1)
    extended = jnp.concatenate([earlier, inputs], 1)
    shifted = [
        lax.dynamic_slice_in_dim(extended, receptive_span - taps[k], time_n, 1)
        for k in range(tap_count)
    ]
    stacked = jnp.concatenate(shifted, 2).reshape(rows, tap_count * width)
    pre = jnp.dot(stacked, wide, preferred_element_type=jnp.float32)
    sig = jax.nn.sigmoid(pre)
    upstream = cotangent.reshape(rows, width)
    dpre_flat = (upstream.astype(jnp.float32) * (sig * (1.0 + pre * (1.0 - sig)))).astype(
        jnp.bfloat16
    )
    dpre = dpre_flat.reshape(series_n, time_n, width)
    ahead = passed_along(dpre[:, :receptive_span, :], "tm", -1)
    later = jnp.concatenate([dpre, ahead], 1)
    result = upstream.astype(jnp.float32)
    for k in range(tap_count):
        moved = lax.dynamic_slice_in_dim(later, taps[k], time_n, 1).reshape(rows, width)
        result = result + lax.dot_general(
            moved,
            wide[k * width : (k + 1) * width],
            (((1,), (1,)), ((), ())),
            preferred_element_type=jnp.float32,
        )
    grad_input = result.astype(jnp.bfloat16).reshape(series_n, time_n, width)
    grad_shard = lax.psum_scatter(
        lax.dot_general(
            stacked, dpre_flat, (((0,), (0,)), ((), ())), preferred_element_type=jnp.float32
        ),
        "series",
        scatter_dimension=0,
        tiled=True,
    )
    grad_shard = lax.psum(grad_shard, "tm")
    new_weight, new_moment_one, new_moment_two = adamw(
        weight, grad_shard, moment_one, second_moment_state
    )
    return (grad_input, new_weight, new_moment_one, new_moment_two)


MESH = pl.DeviceIdType.MESH
F32, BF16 = jnp.float32, jnp.bfloat16
PLANES, IN_PLANE = 4, 8


def fits(mesh):
    return mesh.shape["tm"] == 1 and mesh.shape["series"] == PLANES * IN_PLANE


def matmul(a, b):
    return jnp.dot(a, b, preferred_element_type=F32)


def matmul_t(a, b):
    return lax.dot_general(a, b, (((1,), (1,)), ((), ())), preferred_element_type=F32)


def kernel(
    taps_ref, x_hbm, cot_hbm, w_hbm, gi_hbm, grad_hbm,
    x, cot, w, gi, grad_ref,
    wide, xs, xt, pre, dk, g, s1, r1, s2, r2, s3, r3,
    load_sem, store_sem, ag_send, ag_recv, rs_send, rs_recv,
):
    series_n, time_n, width = x.shape
    flat = series_n * time_n
    span = 2 * DILATION_GAP
    rows = w.shape[0]
    group = IN_PLANE * rows
    half = width // 2
    tm = lax.axis_index("tm")
    me = lax.axis_index("series")
    core = lax.rem(me, 2)
    px = lax.rem(me // 2, 2)
    py = lax.rem(me // 4, 2)
    z = me // IN_PLANE

    def index(zz, yy, xx, cc):
        return ((zz * 2 + yy) * 2 + xx) * 2 + cc

    def block(zz, yy, xx, cc):
        return pl.ds(pl.multiple_of(index(zz, yy, xx, cc) * rows, 16), rows)

    to_x = (tm, index(z, py, 1 - px, core))
    to_y = (tm, index(z, 1 - py, px, core))
    to_d = (tm, index(z, 1 - py, 1 - px, core))
    to_c = (tm, index(z, py, px, 1 - core))
    to_z = [None] + [(tm, index(lax.rem(z + d, PLANES), py, px, core)) for d in (1, 2, 3)]

    loads = [
        pltpu.make_async_copy(src, dst, load_sem.at[i])
        for i, (src, dst) in enumerate([(w_hbm, w), (x_hbm, x), (cot_hbm, cot)])
    ]
    loads[0].start()

    barrier = pltpu.get_barrier_semaphore()
    for dev in (to_x, to_y, to_d, to_c, *to_z[1:]):
        pl.semaphore_signal(barrier, inc=1, device_id=dev, device_id_type=MESH)

    loads[0].wait()
    own = block(z, py, px, core)
    wide[own, :] = w[...].astype(BF16)

    pl.semaphore_wait(barrier, 7)

    def start(src, dst, sems, k, dev):
        c = pltpu.make_async_remote_copy(
            src_ref=src, dst_ref=dst, send_sem=sems[0].at[k], recv_sem=sems[1].at[k],
            device_id=dev, device_id_type=MESH,
        )
        c.start()
        return c

    ag = (ag_send, ag_recv)
    rs = (rs_send, rs_recv)

    def pass_on(blk, k, dev):
        return start(wide.at[blk, :], wide.at[blk, :], ag, k, dev)

    def before(j):
        return lax.rem(z + PLANES - j, PLANES)

    z_in = [None] + [pass_on(own, d, to_z[d]) for d in (1, 2, 3)]
    plane = [(to_x, py, 1 - px), (to_y, 1 - py, px), (to_d, 1 - py, 1 - px)]
    p_in, c_in = [], [[], [], [], []]

    def first_hop(j):
        if j:
            z_in[j].wait_recv()
        blk = block(before(j), py, px, core)
        p_in.append([pass_on(blk, 4 + 4 * i + j, to) for i, (to, _, _) in enumerate(plane)])
        c_in[j].append(pass_on(blk, 16 + j, to_c))

    def second_hop(j):
        for i, (_, yy, xx) in enumerate(plane):
            p_in[j][i].wait_recv()
            c_in[j].append(pass_on(block(before(j), yy, xx, core), 20 + 4 * i + j, to_c))

    def forward(j):
        for c in c_in[j]:
            c.wait_recv()
        at = pl.ds(pl.multiple_of(before(j) * group, 128), group)
        term = matmul(xs[:, at], wide[at, :])
        pre[...] = term if j == 0 else pre[...] + term

    first_hop(0)
    loads[1].start()
    tap = taps_ref[1]
    row = lax.broadcasted_iota(jnp.int32, (time_n, time_n), 0)
    column = lax.broadcasted_iota(jnp.int32, (time_n, time_n), 1)
    back = jnp.where(column == row - tap, 1.0, 0.0).astype(BF16)
    ahead = jnp.where(column == row + tap, 1.0, 0.0).astype(BF16)
    taps_at = [pl.ds(k * width, width) for k in range(3)]

    def shift(s):
        first = s * time_n
        at = pl.ds(first, time_n)
        xs[at, taps_at[0]] = x[s]
        xs[at, taps_at[1]] = matmul(back, x[s]).astype(BF16)
        xs[pl.ds(first, span), taps_at[2]] = jnp.zeros((span, width), BF16)
        xs[pl.ds(first + span, time_n - span), taps_at[2]] = x[s, pl.ds(0, time_n - span), :]

    def transpose(s, h):
        first = s * time_n
        at = pl.ds(first, time_n)
        turned = x[s, :, pl.ds(h * half, half)].T
        xt[pl.ds(h * half, half), at] = turned
        xt[pl.ds(width + h * half, half), at] = xs[at, pl.ds(width + h * half, half)].T
        last = pl.ds(2 * width + h * half, half)
        xt[last, pl.ds(first, span)] = jnp.zeros((half, span), BF16)
        xt[last, pl.ds(first + span, time_n - span)] = turned[:, : time_n - span]

    first_hop(1)
    loads[1].wait()
    loads[2].start()
    shift(0)
    first_hop(2)
    transpose(0, 0)
    first_hop(3)
    second_hop(0)
    shift(1)
    second_hop(1)
    transpose(0, 1)
    forward(0)
    second_hop(2)
    transpose(1, 0)
    forward(1)
    second_hop(3)
    transpose(1, 1)
    forward(2)
    loads[2].wait()
    for c in c_in[3]:
        c.wait_recv()
    at = pl.ds(pl.multiple_of(before(3) * group, 128), group)
    step = 256
    fine = 32
    for first in range(0, flat, step):
        part = pl.ds(first, step)
        total = pre[part, :] + matmul(xs[part, at], wide[at, :])
        for f in range(0, step, fine):
            t = total[f : f + fine]
            sig = 0.5 * jnp.tanh(0.5 * t) + 0.5
            up = cot[first // time_n, pl.ds(first % time_n + f, fine), :].astype(F32)
            dk[0, pl.ds(first + f, fine), :] = (up * (sig * (1.0 + t * (1.0 - sig)))).astype(BF16)

    c1, p2, z4 = {}, {}, {}

    def after(d):
        return lax.rem(z + d, PLANES)

    def weight_grad(d):
        zz = after(d)
        at = pl.ds(pl.multiple_of(zz * group, 128), group)
        g[at, :] = matmul(xt[at, :], dk[0])
        for q in range(4):
            s1[d, q] = g[block(zz, q // 2, q % 2, 1 - core), :].astype(BF16)
        c1[d] = start(s1.at[d], r1.at[d], rs, d, to_c)

    def chip_sum(d, yy, xx):
        return g[block(after(d), yy, xx, core), :] + r1[d, yy * 2 + xx].astype(F32)

    def reduce_one(d):
        c1[d].wait_recv()
        p2[d] = []
        for i, (to, yy, xx) in enumerate(plane):
            s2[d, i] = chip_sum(d, yy, xx).astype(BF16)
            p2[d].append(start(s2.at[d, i], r2.at[d, i], rs, 4 + 3 * d + i, to))

    def reduce_two(d):
        total = chip_sum(d, py, px)
        for i in range(3):
            p2[d][i].wait_recv()
            total = total + r2[d, i].astype(F32)
        if d:
            s3[d - 1] = total.astype(BF16)
            z4[d] = start(s3.at[d - 1], r3.at[d - 1], rs, 15 + d, to_z[d])
        else:
            grad_ref[...] = total

    stores = []

    def shift_dpre(s):
        first = s * time_n
        dk[1, pl.ds(first, time_n), :] = matmul(ahead, dk[0, pl.ds(first, time_n), :]).astype(BF16)

    def static_shift_dpre(s):
        first = s * time_n
        dk[2, pl.ds(first, time_n - span), :] = dk[0, pl.ds(first + span, time_n - span), :]
        dk[2, pl.ds(first + time_n - span, span), :] = jnp.zeros((span, width), BF16)

    def grad_input(k):
        term = matmul_t(dk[k], wide[taps_at[k], :])
        for s in range(series_n):
            part = pl.ds(s * time_n, time_n)
            mine = term[s * time_n : (s + 1) * time_n]
            if k == 0:
                pre[part, :] = cot[s].astype(F32) + mine
            elif k == 2:
                pre[part, :] = pre[part, :] + mine
            else:
                gi[s] = (pre[part, :] + mine).astype(BF16)
                c = pltpu.make_async_copy(gi.at[s], gi_hbm.at[s], store_sem.at[s])
                c.start()
                stores.append(c)

    o = (2, 1, 3, 0)
    weight_grad(o[0])
    weight_grad(o[1])
    reduce_one(o[0])
    weight_grad(o[2])
    reduce_one(o[1])
    weight_grad(o[3])
    reduce_one(o[2])
    reduce_one(o[3])
    grad_input(0)
    reduce_two(o[0])
    for s in range(series_n):
        static_shift_dpre(s)
    grad_input(2)
    reduce_two(o[1])
    for s in range(series_n):
        shift_dpre(s)
    reduce_two(o[2])
    reduce_two(o[3])
    grad_input(1)
    total = grad_ref[...]
    for d in (2, 1, 3):
        z4[d].wait_recv()
        total = total + r3[d - 1].astype(F32)
    grad_ref[...] = total
    c = pltpu.make_async_copy(grad_ref, grad_hbm, store_sem.at[series_n])
    c.start()
    stores.append(c)
    for c in z_in[1:] + sum(p_in, []) + sum(c_in, []) + sum(p2.values(), []):
        c.wait_send()
    for made in (c1, z4):
        for c in made.values():
            c.wait_send()
    for c in stores:
        c.wait()


def finish(
    gi, grad, weight, moment_one, second_moment_state, gi_out, nw_out, n1_out, n2_out,
    held, state, new, in_sem, out_sem, state_sem, new_sem,
):
    parts = [(s, pl.ds(h * held.shape[1] // 2, held.shape[1] // 2)) for s in range(held.shape[0]) for h in range(2)]
    inward = [pltpu.make_async_copy(gi.at[p], held.at[p], in_sem.at[i]) for i, p in enumerate(parts)]
    states = [
        pltpu.make_async_copy(src, state.at[i], state_sem.at[i])
        for i, src in enumerate((weight, grad, moment_one, second_moment_state))
    ]
    for c in inward + states:
        c.start()
    outward = []
    for i, p in enumerate(parts):
        inward[i].wait()
        outward.append(pltpu.make_async_copy(held.at[p], gi_out.at[p], out_sem.at[i]))
        outward[-1].start()
    for c in states:
        c.wait()
    new[0], new[1], new[2] = adamw(state[0], state[1], state[2], state[3])
    for i, dst in enumerate((nw_out, n1_out, n2_out)):
        outward.append(pltpu.make_async_copy(new.at[i], dst, new_sem.at[i]))
        outward[-1].start()
    for c in outward:
        c.wait()


def fused(inputs, cotangent, taps, weight, moment_one, second_moment_state):
    series_n, time_n, width = inputs.shape
    rows = weight.shape[0]
    depth = taps.shape[0] * width
    flat = series_n * time_n
    state = jax.ShapeDtypeStruct(weight.shape, F32)
    hbm = pl.BlockSpec(memory_space=pltpu.HBM)
    V = pltpu.VMEM
    gi, grad = pl.pallas_call(
        kernel,
        out_shape=[jax.ShapeDtypeStruct(inputs.shape, BF16), state],
        in_specs=[pl.BlockSpec(memory_space=pltpu.SMEM)] + [hbm] * 3,
        out_specs=[hbm] * 2,
        scratch_shapes=[
            V(inputs.shape, BF16), V(inputs.shape, BF16), V(weight.shape, F32),
            V(inputs.shape, BF16), V(weight.shape, F32),
            V((depth, width), BF16),
            V((flat, depth), BF16),
            V((depth, flat), BF16),
            V((flat, width), F32),
            V((3, flat, width), BF16),
            V((depth, width), F32),
            V((PLANES, 4, rows, width), BF16), V((PLANES, 4, rows, width), BF16),
            V((PLANES, 3, rows, width), BF16), V((PLANES, 3, rows, width), BF16),
            V((3, rows, width), BF16), V((3, rows, width), BF16),
            pltpu.SemaphoreType.DMA((3,)), pltpu.SemaphoreType.DMA((series_n + 1,)),
            pltpu.SemaphoreType.DMA((32,)), pltpu.SemaphoreType.DMA((32,)),
            pltpu.SemaphoreType.DMA((19,)), pltpu.SemaphoreType.DMA((19,)),
        ],
        compiler_params=pltpu.CompilerParams(
            collective_id=0, has_side_effects=True, vmem_limit_bytes=63 * 1024 * 1024
        ),
        cost_estimate=pl.CostEstimate(
            flops=6 * flat * depth * width, bytes_accessed=6 * flat * width, transcendentals=flat * width
        ),
    )(taps, inputs, cotangent, weight)
    return tuple(pl.pallas_call(
        finish,
        out_shape=[jax.ShapeDtypeStruct(inputs.shape, BF16), state, state, state],
        in_specs=[hbm] * 5,
        out_specs=[hbm] * 4,
        scratch_shapes=[
            V(inputs.shape, BF16), V((4, rows, width), F32), V((3, rows, width), F32),
            pltpu.SemaphoreType.DMA((2 * series_n,)), pltpu.SemaphoreType.DMA((2 * series_n,)),
            pltpu.SemaphoreType.DMA((4,)), pltpu.SemaphoreType.DMA((3,)),
        ],
        compiler_params=pltpu.CompilerParams(vmem_limit_bytes=63 * 1024 * 1024),
        cost_estimate=pl.CostEstimate(flops=20 * rows * width, bytes_accessed=28 * rows * width, transcendentals=0),
    )(gi, grad, weight, moment_one, second_moment_state))


def solution(mesh):
    in_specs = (
        P("series", "tm", None),
        P("series", "tm", None),
        P(),
        P("series", None),
        P("series", None),
        P("series", None),
    )
    out_specs = (P("series", "tm", None), P("series", None), P("series", None), P("series", None))
    step = fused if fits(mesh) else body
    return jax.shard_map(step, mesh=mesh, in_specs=in_specs, out_specs=out_specs, check_vma=False)
```
